256 devices in a mesh: ctx: 32 (over x_lo, z, core), exp: 8 (over x_hi, y).
Axes of the slice: x: 4 (x_hi: 2, x_lo: 2; x = x_hi * 2 + x_lo), y: 4, z: 8, core: 2. Of those that a mesh axis runs over, the one named last changes fastest.
Arguments:
- queries: bfloat16 [3072, 4096], P('ctx', 'exp'), may hold values from -8 to 8
- keys: bfloat16 [3072, 1024], P('ctx', 'exp'), may hold values from -6 to 6
- values: bfloat16 [3072, 1024], P('ctx', 'exp'), may hold values from -6 to 6
- out_weight: bfloat16 [4096, 4096], P('exp', 'ctx'), may hold values from -0.09375 to 0.09375
- residual: bfloat16 [3072, 4096], P(('ctx', 'exp')), may hold values from -6 to 6
- norm_gain: float32 [4096], replicated, may hold values from 0.25 to 2.5
- gate_weight: bfloat16 [8, 4096, 12288], P('exp', None, 'ctx'), may hold values from -0.09375 to 0.09375
- up_weight: bfloat16 [8, 4096, 12288], P('exp', None, 'ctx'), may hold values from -0.09375 to 0.09375
- down_weight: bfloat16 [8, 12288, 4096], P('exp', 'ctx'), may hold values from -0.0546875 to 0.0546875
- route_ids: int32 [3072, 2], P(('ctx', 'exp')), may hold values from 0 to 7, all different within a row; in each aligned block of 12 rows (0 to 11, 12 to 23, ...) at most 6 rows name the same one
- route_weight: float32 [3072, 2], P(('ctx', 'exp')), may hold values from 0.2 to 1
Outputs:
- block_out: bfloat16 [3072, 4096], P(('ctx', 'exp'))
The draws below stay inside these ranges and needn't reach their ends.
Inputs may be any that keep to these rules, and one draw needn't show every extreme that they name: `route_ids`: each row names 2 different experts. Within the 12 rows of one device no expert is named by more than 6 rows, and in some device's rows an expert is named by exactly 6.
All inputs are finite; a program needn't handle non-finite values.
Results may differ from the reference program's by a relative error of at most 0.029.
Values may be sent and summed in bfloat16 or wider, within the bound.
No kernel may reach another device: no remote copies, remote signals or barrier semaphores. Data moves between devices by JAX's collectives and lax.ppermute only.
A program may use at most 128 MiB of HBM per device.

```python
import math
import jax
import jax.numpy as jnp
import numpy as np
from jax import lax

D = 4096
QH = 32
KVH = 8
HD = 128
FF = 12288
EXPERTS = 8
TOP = 2
SEQ = 3072
TOK_DEV = 12
CAP = 6
N_CTX = 32
N_EXP = 8


def draw_keys(key, part):
    key = jax.random.fold_in(key, 11)
    base = jnp.clip(jax.random.normal(key, (SEQ, KVH, HD), jnp.float32), -6.0, 6.0)
    return base.reshape(SEQ, KVH * HD).astype(jnp.bfloat16)


def draw_queries(key, part):
    key = jax.random.fold_in(key, 12)
    base = jnp.clip(2.0 * jax.random.normal(key, (SEQ, QH, HD), jnp.float32), -8.0, 8.0)
    return base.reshape(SEQ, QH * HD).astype(jnp.bfloat16)


def levels(own_key, extent, split, smallest, largest):
    gain = 1.0
    for dim, parts in split:
        draws = jax.random.uniform(jax.random.fold_in(jax.random.fold_in(own_key, 6), dim), (parts,), jnp.float32, smallest / len(split), largest / len(split))
        gain = gain * jnp.repeat(jnp.exp(draws), extent[dim] // parts).reshape((-1,) + (1,) * (len(extent) - 1 - dim))
    return gain


def shared_out(rng, own, number, rows, count, top, limit, lean):
    order = jax.random.permutation(rng, count)
    packed, ordinary = load_shares(count, rows * top, limit, lean, True), load_shares(count, rows * top, limit, lean, False)
    places = jnp.arange(count)

    def named(lengths, offset_by):
        used = int((lengths > 0).sum())
        fixed = max(1, used // 4)
        passed = fixed + (places - fixed + offset_by * (used - fixed)) % max(1, count - fixed)
        return jnp.zeros((count,), jnp.int32).at[order[jnp.where(places < fixed, places, passed)]].set(jnp.asarray(lengths, jnp.int32))

    lengths = jnp.where(number % 4 == 0, named(packed, number // 4), named(ordinary, number - number // 4 - 1))
    mixed = jax.random.permutation(jax.random.fold_in(own, 3), count)
    source_of, receiver = mixed[0:count // 2 * 2:2], mixed[1:count // 2 * 2:2]
    margin = jnp.minimum(lengths[source_of] - 1, limit - lengths[receiver]) // 2
    margin = jnp.where((source_of == order[0]) | (receiver == order[0]) | (lengths[receiver] == 0), 0, jnp.maximum(margin, 0))
    passed = jax.random.randint(jax.random.fold_in(own, 4), (count // 2,), 0, 1 << 20) % (margin + 1)
    lengths = lengths.at[source_of].add(-passed).at[receiver].add(passed)
    members = jnp.searchsorted(jnp.cumsum(lengths), jnp.arange(rows * top), side="right").astype(jnp.int32)
    listing = members.reshape(top, rows).T
    listing = listing[jax.random.permutation(jax.random.fold_in(own, 1), rows)]
    offset_by = jax.random.randint(jax.random.fold_in(own, 2), (rows, 1), 0, top)
    return jnp.take_along_axis(listing, (jnp.arange(top)[None, :] + offset_by) % top, axis=1)


def load_shares(amount, total, most, skew, full):
    weights = [(1 << 20) // math.isqrt(standing ** skew) + 1 for standing in range(1, amount + 1)]
    largest = most if full else min(most, max(-(-total // amount), total * weights[0] // sum(weights)))
    least = 1 if total - largest >= amount - 1 else 0
    holding, spare = [largest] + [least] * (amount - 1), total - largest - least * (amount - 1)
    while spare > 0:
        free = [i for i in range(1, amount) if holding[i] < largest] or [i for i in range(1, amount) if holding[i] < most]
        mass, left = sum([weights[i] for i in free]), spare
        for i in free:
            more = min(most - holding[i], max(1, left * weights[i] // mass), spare)
            holding[i] = holding[i] + more
            spare = spare - more
    return np.array(holding)


def noise(key, dims, spread, most, pieces=(), kind=jnp.bfloat16):
    array = jax.random.normal(key, dims, jnp.float32) * spread
    if len(pieces) > 0:
        array = levels(key, dims, pieces, -0.22, 0.18) * array
    return jnp.clip(array, min=-most, max=most).astype(kind)


def setup_inputs(seed: int = 0) -> dict:
    seeds = jax.random.split(jax.random.key(seed), 12)
    queries = draw_queries(jax.random.fold_in(seeds[11], 71), 0)
    keys = draw_keys(jax.random.fold_in(seeds[11], 71), 0)
    values = noise(seeds[2], (SEQ, KVH * HD), 1.0, 6.0, ((0, 32), (1, 8)))
    out_weight = noise(seeds[3], (QH * HD, D), (QH * HD) ** -0.5, 0.09375, ((0, 8), (1, 32)))
    residual = noise(seeds[4], (SEQ, D), 1.0, 6.0, ((0, 256),))
    norm_gain = jnp.clip(jnp.exp(jax.random.uniform(seeds[5], (D,), jnp.float32, math.log(0.25), math.log(2.5))), 0.25, 2.5)
    gate_weight = noise(seeds[6], (EXPERTS, D, FF), D ** -0.5, 0.09375, ((0, 8), (2, 32)))
    up_weight = noise(seeds[7], (EXPERTS, D, FF), D ** -0.5, 0.09375, ((0, 8), (2, 32)))
    down_weight = noise(seeds[8], (EXPERTS, FF, D), FF ** -0.5, 0.0546875, ((0, 8), (1, 32)))
    route_ids_keys = jax.random.split(jax.random.fold_in(seeds[9], 1), SEQ // TOK_DEV)
    route_ids_turns = jax.random.permutation(jax.random.fold_in(seeds[9], 3), SEQ // TOK_DEV)
    route_ids = jax.vmap(lambda own, number: shared_out(jax.random.fold_in(seeds[9], 2), own, number, TOK_DEV, EXPERTS, TOP, CAP, 2))(route_ids_keys, route_ids_turns).reshape((SEQ, TOP))
    route_weight = jnp.clip(0.2 + 0.8 * jax.random.uniform(seeds[10], (SEQ, TOP), jnp.float32) ** levels(seeds[10], (SEQ, TOP), ((0, 256),), -0.2, 0.2), 0.2, 1.0)
    return dict(queries=queries, keys=keys, values=values, out_weight=out_weight, residual=residual, norm_gain=norm_gain, gate_weight=gate_weight, up_weight=up_weight, down_weight=down_weight, route_ids=route_ids, route_weight=route_weight)


def reference(queries, keys, values, out_weight, residual, norm_gain, gate_weight, up_weight, down_weight, route_ids, route_weight):
    group = QH // KVH
    q_heads = queries.reshape(SEQ, QH, HD)
    k_heads = keys.reshape(SEQ, KVH, HD)
    v_heads = values.reshape(SEQ, KVH, HD)
    position = jnp.arange(SEQ, dtype=jnp.int32)
    causal = position[:, None] >= position[None, :]
    scale = 1.0 / math.sqrt(HD)

    def one_head(head):
        kv_head = head // group
        query = lax.dynamic_index_in_dim(q_heads, head, 1, keepdims=False)
        key_h = lax.dynamic_index_in_dim(k_heads, kv_head, 1, keepdims=False)
        value_per_head = lax.dynamic_index_in_dim(v_heads, kv_head, 1, keepdims=False)
        scores = jnp.dot(query, key_h.T, preferred_element_type=jnp.float32) * scale
        scores = jnp.where(causal, scores, -jnp.inf)
        probs = jax.nn.softmax(scores, axis=-1).astype(jnp.bfloat16)
        return jnp.dot(probs, value_per_head, preferred_element_type=jnp.float32).astype(jnp.bfloat16)
    heads = lax.map(one_head, jnp.arange(QH, dtype=jnp.int32))
    heads = heads.transpose(1, 0, 2).reshape(SEQ, QH * HD)
    attn = jnp.dot(heads, out_weight, preferred_element_type=jnp.float32)
    hstate = residual.astype(jnp.float32) + attn
    meansq = lax.optimization_barrier(jnp.mean(hstate * hstate, axis=-1, keepdims=True))
    normed = (hstate * lax.rsqrt(meansq + 1e-05) * norm_gain).astype(jnp.bfloat16)
    flat_ids = route_ids.reshape(-1)
    flat_weight = route_weight.reshape(-1)
    bound = N_CTX * N_EXP * CAP
    panel = FF // N_CTX

    def expert_pass(mixed, expert):
        chosen = flat_ids == expert
        selected_experts = jnp.nonzero(chosen, size=bound, fill_value=0)[0].astype(jnp.int32)
        valid = jnp.arange(bound, dtype=jnp.int32) < jnp.sum(chosen.astype(jnp.int32))
        token = selected_experts // TOP
        rows = normed[token]
        w_gate = lax.dynamic_index_in_dim(gate_weight, expert, 0, keepdims=False)
        w_up = lax.dynamic_index_in_dim(up_weight, expert, 0, keepdims=False)
        w_down = lax.dynamic_index_in_dim(down_weight, expert, 0, keepdims=False)
        gate = jnp.dot(rows, w_gate, preferred_element_type=jnp.float32)
        upper = jnp.dot(rows, w_up, preferred_element_type=jnp.float32)
        act = (jax.nn.silu(gate) * upper).astype(jnp.bfloat16)

        def add_panel(total, index):
            piece = lax.dynamic_slice_in_dim(act, index * panel, panel, 1)
            weights = lax.dynamic_slice_in_dim(w_down, index * panel, panel, 0)
            part = jnp.dot(piece, weights, preferred_element_type=jnp.float32).astype(jnp.bfloat16)
            part = lax.optimization_barrier(part)
            return (total + part.astype(jnp.float32), None)
        summed, _ = lax.scan(add_panel, jnp.zeros((bound, D), jnp.float32), jnp.arange(N_CTX, dtype=jnp.int32))
        rounded = lax.optimization_barrier(summed.astype(jnp.bfloat16)).astype(jnp.float32)
        scaled = jnp.where(valid, flat_weight[selected_experts], 0.0)
        mixed = mixed.at[token].add(scaled[:, None] * rounded)
        return (mixed, None)
    mixed, _ = lax.scan(expert_pass, jnp.zeros((SEQ, D), jnp.float32), jnp.arange(EXPERTS, dtype=jnp.int32))
    return (hstate + mixed).astype(jnp.bfloat16)
```

```python
import math

import jax
import jax.numpy as jnp
from jax import lax
from jax.sharding import Mesh
from jax.sharding import PartitionSpec as P

HD = 128
EXPERTS = 8
NX, NZ, NC, NH, NY = 2, 8, 2, 2, 4
CTX = ("xl", "z", "c")
EXP = ("xh", "y")
SWAP = [(0, 1), (1, 0)]
bf16 = jnp.bfloat16
f32 = jnp.float32


def zshift(x, by):
    return lax.ppermute(x, "z", [(i, (i + by) % NZ) for i in range(NZ)])


def ring_gather(x):
    half = x.shape[0] // 2
    out = [None] * NZ
    out[0] = x
    f = b = x
    for s in range(1, NZ // 2):
        f = zshift(f, 1)
        b = zshift(b, -1)
        out[-s % NZ] = f
        out[s] = b
    out[NZ // 2] = jnp.concatenate([zshift(f[:half], 1), zshift(b[half:], -1)], axis=0)
    return out


def ring_reduce(parts):
    half = parts[0].shape[0] // 2
    far = parts[NZ // 2]
    f = zshift(far[:half], 1)
    b = zshift(far[half:], -1)
    first = True
    for s in range(NZ // 2 - 1, 0, -1):
        up, down = parts[s].astype(f32), parts[-s % NZ].astype(f32)
        if first:
            up = jnp.concatenate([up[:half] + f.astype(f32), up[half:]], axis=0)
            down = jnp.concatenate([down[:half], down[half:] + b.astype(f32)], axis=0)
            first = False
        else:
            up = up + f.astype(f32)
            down = down + b.astype(f32)
        f = zshift(up.astype(bf16), 1)
        b = zshift(down.astype(bf16), -1)
    return parts[0].astype(f32) + f.astype(f32) + b.astype(f32)


def shards(
    queries,
    keys,
    values,
    out_weight,
    residual,
    norm_gain,
    gate_weight,
    up_weight,
    down_weight,
    route_ids,
    route_weight,
):
    xl, z, c = lax.axis_index("xl"), lax.axis_index("z"), lax.axis_index("c")
    tok_blk = queries.shape[0]
    group = queries.shape[1] // HD
    width = residual.shape[1]
    ctx = (xl * NZ + z) * NC + c
    block_first = ctx * tok_blk

    def other_x(x):
        return lax.ppermute(x, "xl", SWAP)

    def other_core(x):
        return lax.ppermute(x, "c", SWAP)

    kv = jnp.concatenate([keys, values], axis=1)
    pair = jnp.concatenate([kv, other_x(kv)], axis=0)
    mine = jnp.concatenate(ring_gather(pair), axis=0)
    kv_all = jnp.concatenate([mine, other_core(mine)], axis=0)
    core_of = jnp.stack([c, 1 - c])[:, None, None, None]
    z_of = ((z + jnp.arange(NZ, dtype=jnp.int32)) % NZ)[None, :, None, None]
    x_of = jnp.stack([xl, 1 - xl])[None, None, :, None]
    k_position = (
        ((x_of * NZ + z_of) * NC + core_of) * tok_blk
        + jnp.arange(tok_blk, dtype=jnp.int32)[None, None, None, :]
    ).reshape(-1)

    ow_pair = jnp.concatenate([out_weight, other_x(out_weight)], axis=1)
    ow_mine = jnp.concatenate(ring_gather(ow_pair), axis=1)
    ow_other = other_core(ow_mine)

    gate_o, up_o, down_o = other_core(gate_weight[0]), other_core(up_weight[0]), other_core(down_weight[0])

    q = queries.reshape(tok_blk, group, HD)
    q_position = block_first + jnp.arange(tok_blk, dtype=jnp.int32)
    scores = jnp.einsum("wvn,un->vwu", q, kv_all[:, :HD], preferred_element_type=f32) * (
        1.0 / math.sqrt(HD)
    )
    allowed = k_position[None, :] <= q_position[:, None]
    scores = jnp.where(allowed, scores, -1e30)
    top = jnp.max(scores, axis=-1, keepdims=True)
    weights = jnp.where(allowed, jnp.exp(scores - top), 0.0)
    total = jnp.sum(weights, axis=-1, keepdims=True)
    acc = jnp.einsum("cej,ji->cei", weights.astype(bf16), kv_all[:, HD:], preferred_element_type=f32)
    heads = (acc / total).transpose(1, 0, 2).reshape(tok_blk, group * HD).astype(bf16)

    part = jnp.concatenate(
        [
            jnp.dot(heads, ow_mine, preferred_element_type=f32).astype(bf16),
            jnp.dot(heads, ow_other, preferred_element_type=f32).astype(bf16),
        ],
        axis=1,
    )
    tok_dev = residual.shape[0]
    parts = lax.all_to_all(
        part.reshape(EXPERTS, tok_dev, width), EXP, split_axis=0, concat_axis=0, tiled=True
    )
    attn = jnp.sum(parts.astype(f32), axis=0).reshape(tok_dev, NC, NZ, NX, HD)
    attn = jnp.roll(attn, z, axis=2)
    attn = jnp.where(c == 0, attn, attn[:, ::-1])
    attn = jnp.where(xl == 0, attn, attn[:, :, :, ::-1])
    attn = attn.transpose(0, 3, 2, 1, 4).reshape(tok_dev, width)

    hstate = residual.astype(f32) + attn
    meansq = jnp.mean(hstate * hstate, axis=-1, keepdims=True)
    normed = (hstate * lax.rsqrt(meansq + 1e-05) * norm_gain).astype(bf16)

    picks = route_ids.shape[1]
    cap = 2 * tok_dev * picks // EXPERTS
    flat_ids = route_ids.reshape(-1)
    onehot = (flat_ids[:, None] == jnp.arange(EXPERTS, dtype=jnp.int32)[None, :]).astype(jnp.int32)
    earlier = jnp.cumsum(onehot, axis=0) - onehot
    slot = jnp.sum(earlier * onehot, axis=1)
    place = flat_ids * cap + slot
    hits = (
        jnp.arange(EXPERTS * cap, dtype=jnp.int32)[None, :] == place[:, None]
    ).reshape(tok_dev, picks, EXPERTS * cap)
    placing = jnp.any(hits, axis=1).astype(bf16)
    combine = jnp.sum(
        jnp.where(hits, route_weight[:, :, None], 0.0), axis=1
    )
    outgoing = (
        lax.dot_general(placing, normed, (((0,), (0,)), ((), ())), preferred_element_type=f32)
        .astype(bf16)
        .reshape(EXPERTS, cap, width)
    )
    rows = lax.all_to_all(outgoing, EXP, split_axis=0, concat_axis=0, tiled=True).reshape(
        EXPERTS * cap, width
    )
    rows = jnp.concatenate([rows, other_x(rows)], axis=0)

    def experts(x):
        outs = 0.0
        for g, u, d in ((gate_weight[0], up_weight[0], down_weight[0]), (gate_o, up_o, down_o)):
            gate = jnp.dot(x, g, preferred_element_type=f32)
            upper = jnp.dot(x, u, preferred_element_type=f32)
            act = (jax.nn.silu(gate) * upper).astype(bf16)
            outs = outs + jnp.dot(act, d, preferred_element_type=f32)
        return outs.astype(bf16)

    arrived = ring_gather(rows)
    done = [None] * NZ
    done[0] = experts(arrived[0])
    for s in range(1, NZ // 2):
        both = experts(jnp.concatenate([arrived[s], arrived[NZ - s]], axis=0))
        done[s], done[NZ - s] = both[: rows.shape[0]], both[rows.shape[0] :]
    done[NZ // 2] = experts(arrived[NZ // 2])
    summed = ring_reduce(done)
    n = EXPERTS * cap
    mixed_rows = (summed[:n] + other_x(summed[n:].astype(bf16)).astype(f32)).astype(bf16)
    back = lax.all_to_all(
        mixed_rows.reshape(EXPERTS, cap, width), EXP, split_axis=0, concat_axis=0, tiled=True
    ).reshape(n, width)
    mixed = jnp.dot(
        combine,
        back.astype(f32),
        precision=lax.Precision.HIGHEST,
        preferred_element_type=f32,
    )
    return (hstate + mixed).astype(bf16)


def solution(mesh):
    fine = Mesh(mesh.devices.reshape(NX, NZ, NC, NH, NY), CTX + EXP)
    placed = (
        P(CTX, EXP),
        P(CTX, EXP),
        P(CTX, EXP),
        P(EXP, CTX),
        P(CTX + EXP, None),
        P(),
        P(EXP, None, CTX),
        P(EXP, None, CTX),
        P(EXP, CTX, None),
        P(CTX + EXP, None),
        P(CTX + EXP, None),
    )
    return jax.shard_map(
        shards, mesh=fine, in_specs=placed, out_specs=P(CTX + EXP, None), check_vma=False
    )
```

```python
import math

import jax
import jax.numpy as jnp
from jax import lax
from jax.experimental import pallas as pl
from jax.experimental.pallas import tpu as pltpu
from jax.sharding import Mesh
from jax.sharding import PartitionSpec as P

HD = 128
EXPERTS = 8
NX, NZ, NC, NH, NY = 2, 8, 2, 2, 4
CTX = ("xl", "z", "c")
EXP = ("xh", "y")
SWAP = [(0, 1), (1, 0)]
bf16 = jnp.bfloat16
f32 = jnp.float32


HALF = NZ // 2


def even(x):
    return lax.ppermute(x, "z", [(i, i ^ 1) for i in range(NZ)])


def odd(x):
    return lax.ppermute(x, "z", [(i, (i + 1 if i % 2 else i - 1) % NZ) for i in range(NZ)])


def ring_gather(x):
    half = x.shape[0] // 2
    out = [None] * NZ
    out[0] = x
    a = b = x
    for s in range(1, HALF):
        a, b = even(b), odd(a)
        out[s], out[NZ - s] = a, b
    out[HALF] = (even(b[:half]), odd(a[half:]))
    return out


def add(p, q):
    return (p.astype(f32) + q.astype(f32)).astype(bf16)


def ring_reduce(parts):
    half = parts[0].shape[0] // 2
    far = parts[HALF]
    ra, rb = even(far[:half]), odd(far[half:])
    for s in range(HALF - 1, 0, -1):
        pa, pb = parts[s], parts[NZ - s]
        if s == HALF - 1:
            sa = jnp.concatenate([pa[:half], add(pa[half:], rb)], axis=0)
            sb = jnp.concatenate([add(pb[:half], ra), pb[half:]], axis=0)
        else:
            sa, sb = add(pa, rb), add(pb, ra)
        ra, rb = even(sa), odd(sb)
    return parts[0].astype(f32) + ra.astype(f32) + rb.astype(f32)


def experts_kernel(x_ref, g0, u0, d0, g1, u1, d1, o_ref, wg, wu, wd, sem):
    copies = []
    for p, (g, u, d) in enumerate(((g0, u0, d0), (g1, u1, d1))):
        for k, (src, dst) in enumerate(((g, wg), (u, wu), (d, wd))):
            copies.append(pltpu.make_async_copy(src, dst.at[p], sem.at[3 * p + k]))
    for copy in copies:
        copy.start()
    x = x_ref[...]
    out = None
    for p in range(2):
        copies[3 * p].wait()
        gate = jnp.dot(x, wg[p], preferred_element_type=f32)
        copies[3 * p + 1].wait()
        upper = jnp.dot(x, wu[p], preferred_element_type=f32)
        act = (gate / (1.0 + jnp.exp(-gate)) * upper).astype(bf16)
        copies[3 * p + 2].wait()
        down = jnp.dot(act, wd[p], preferred_element_type=f32)
        out = down if out is None else out + down
    o_ref[...] = out.astype(bf16)


def run_experts(x, weights):
    rows, width = x.shape
    ff = weights[0].shape[1]
    hbm = pl.BlockSpec(memory_space=pl.ANY)
    vmem = pl.BlockSpec(memory_space=pltpu.VMEM)
    return pl.pallas_call(
        experts_kernel,
        out_shape=jax.ShapeDtypeStruct((rows, width), bf16),
        in_specs=[vmem] + [hbm] * 6,
        out_specs=vmem,
        scratch_shapes=[
            pltpu.VMEM((2, width, ff), bf16),
            pltpu.VMEM((2, width, ff), bf16),
            pltpu.VMEM((2, ff, width), bf16),
            pltpu.SemaphoreType.DMA((6,)),
        ],
        compiler_params=pltpu.CompilerParams(vmem_limit_bytes=44 * 1024 * 1024),
        cost_estimate=pl.CostEstimate(
            flops=2 * 6 * rows * width * ff,
            bytes_accessed=12 * width * ff + 4 * rows * width,
            transcendentals=2 * rows * ff,
        ),
        name="experts",
    )(x, *weights)


def tail_kernel(src_ref, parts_ref, residual_ref, gain_ref, placing_ref, h_ref, o_ref):
    blocks = h_ref.shape[1] // HD
    for j in range(blocks):
        lanes = pl.ds(pl.multiple_of(src_ref[j] * HD, HD), HD)
        to = slice(j * HD, (j + 1) * HD)
        total = residual_ref[:, to].astype(f32)
        for e in range(EXPERTS):
            total = total + parts_ref[e, :, lanes].astype(f32)
        h_ref[:, to] = total
    h = h_ref[...]
    meansq = jnp.mean(h * h, axis=-1, keepdims=True)
    normed = (h * lax.rsqrt(meansq + 1e-05) * gain_ref[...]).astype(bf16)
    for e in range(EXPERTS):
        o_ref[e] = jnp.dot(placing_ref[e], normed, preferred_element_type=f32).astype(bf16)


def run_tail(src, parts, residual, gain, placing):
    tok, width = residual.shape
    vmem = pl.BlockSpec(memory_space=pltpu.VMEM)
    return pl.pallas_call(
        tail_kernel,
        out_shape=(
            jax.ShapeDtypeStruct((tok, width), f32),
            jax.ShapeDtypeStruct((EXPERTS, placing.shape[1], width), bf16),
        ),
        in_specs=[pl.BlockSpec(memory_space=pltpu.SMEM)] + [vmem] * 4,
        out_specs=(vmem, vmem),
        compiler_params=pltpu.CompilerParams(vmem_limit_bytes=16 * 1024 * 1024),
        name="tail",
    )(src, parts, residual, gain, placing)


def shards(
    queries,
    keys,
    values,
    out_weight,
    residual,
    norm_gain,
    gate_weight,
    up_weight,
    down_weight,
    route_ids,
    route_weight,
):
    xl, z, c = lax.axis_index("xl"), lax.axis_index("z"), lax.axis_index("c")
    tok_blk = queries.shape[0]
    group = queries.shape[1] // HD
    width = residual.shape[1]
    ctx = (xl * NZ + z) * NC + c
    block_first = ctx * tok_blk

    def other_x(x):
        return lax.ppermute(x, "xl", SWAP)

    def other_core(x):
        return lax.ppermute(x, "c", SWAP)

    kv = jnp.concatenate([keys, values], axis=1)
    pair = jnp.concatenate([kv, other_x(kv)], axis=0)
    got = ring_gather(pair)
    mine = jnp.concatenate(got[:HALF] + list(got[HALF]) + got[HALF + 1 :], axis=0)
    kv_all = jnp.concatenate([mine, other_core(mine)], axis=0)
    core_of = jnp.stack([c, 1 - c])[:, None, None, None]
    turn = 1 - 2 * (z % 2)
    z_of = ((z + turn * jnp.arange(NZ, dtype=jnp.int32)) % NZ)[None, :, None, None]
    x_of = jnp.stack([xl, 1 - xl])[None, None, :, None]
    k_position = (
        ((x_of * NZ + z_of) * NC + core_of) * tok_blk
        + jnp.arange(tok_blk, dtype=jnp.int32)[None, None, None, :]
    ).reshape(-1)

    ow_pair = jnp.concatenate([out_weight, other_x(out_weight)], axis=1)
    got = ring_gather(ow_pair)
    got[HALF] = jnp.concatenate(got[HALF], axis=0)
    ow_mine = jnp.concatenate(got, axis=1)
    ow_other = other_core(ow_mine)

    gate_o, up_o, down_o = other_core(gate_weight[0]), other_core(up_weight[0]), other_core(down_weight[0])

    q = queries.reshape(tok_blk, group, HD)
    q_position = block_first + jnp.arange(tok_blk, dtype=jnp.int32)
    scores = jnp.einsum("wvn,un->vwu", q, kv_all[:, :HD], preferred_element_type=f32) * (
        1.0 / math.sqrt(HD)
    )
    allowed = k_position[None, :] <= q_position[:, None]
    scores = jnp.where(allowed, scores, -1e30)
    top = jnp.max(scores, axis=-1, keepdims=True)
    weights = jnp.where(allowed, jnp.exp(scores - top), 0.0)
    total = jnp.sum(weights, axis=-1, keepdims=True)
    acc = jnp.einsum("cej,ji->cei", weights.astype(bf16), kv_all[:, HD:], preferred_element_type=f32)
    heads = (acc / total).transpose(1, 0, 2).reshape(tok_blk, group * HD).astype(bf16)

    heads, gate_o, up_o, down_o = lax.optimization_barrier((heads, gate_o, up_o, down_o))
    part = jnp.concatenate(
        [
            jnp.dot(heads, ow_mine, preferred_element_type=f32).astype(bf16),
            jnp.dot(heads, ow_other, preferred_element_type=f32).astype(bf16),
        ],
        axis=1,
    )
    tok_dev = residual.shape[0]
    parts = lax.all_to_all(
        part.reshape(EXPERTS, tok_dev, width), EXP, split_axis=0, concat_axis=0, tiled=True
    )
    xs = jnp.arange(NX, dtype=jnp.int32)[:, None, None]
    zs = jnp.arange(NZ, dtype=jnp.int32)[None, :, None]
    cs = jnp.arange(NC, dtype=jnp.int32)[None, None, :]
    source = (((cs ^ c) * NZ + (turn * (zs - z)) % NZ) * NX + (xs ^ xl)).reshape(-1)

    picks = route_ids.shape[1]
    cap = 2 * tok_dev * picks // EXPERTS
    flat_ids = route_ids.reshape(-1)
    onehot = (flat_ids[:, None] == jnp.arange(EXPERTS, dtype=jnp.int32)[None, :]).astype(jnp.int32)
    earlier = jnp.cumsum(onehot, axis=0) - onehot
    slot = jnp.sum(earlier * onehot, axis=1)
    place = flat_ids * cap + slot
    hits = (
        jnp.arange(EXPERTS * cap, dtype=jnp.int32)[None, :] == place[:, None]
    ).reshape(tok_dev, picks, EXPERTS * cap)
    placing = jnp.any(hits, axis=1).astype(bf16).T.reshape(EXPERTS, cap, tok_dev)
    combine = jnp.sum(jnp.where(hits, route_weight[:, :, None], 0.0), axis=1)
    hstate, outgoing = run_tail(source, parts, residual, norm_gain[None, :], placing)
    rows = lax.all_to_all(outgoing, EXP, split_axis=0, concat_axis=0, tiled=True).reshape(
        EXPERTS * cap, width
    )
    panels = (gate_weight[0], up_weight[0], down_weight[0], gate_o, up_o, down_o)
    n = rows.shape[0]
    near, over = ring_gather(rows), ring_gather(other_x(rows))
    done_near, done_over = [None] * NZ, [None] * NZ
    both = run_experts(jnp.concatenate([near[0], over[0]], axis=0), panels)
    done_near[0], done_over[0] = both[:n], both[n:]
    for s in range(1, HALF):
        t = NZ - s
        out = run_experts(jnp.concatenate([near[s], near[t], over[s], over[t]], axis=0), panels)
        done_near[s], done_near[t] = out[:n], out[n : 2 * n]
        done_over[s], done_over[t] = out[2 * n : 3 * n], out[3 * n :]
    done_near[HALF] = run_experts(jnp.concatenate(near[HALF], axis=0), panels)
    done_over[HALF] = run_experts(jnp.concatenate(over[HALF], axis=0), panels)
    sum_near, sum_over = ring_reduce(done_near), ring_reduce(done_over)
    mixed_rows = (sum_near + other_x(sum_over.astype(bf16)).astype(f32)).astype(bf16)
    back = lax.all_to_all(
        mixed_rows.reshape(EXPERTS, cap, width), EXP, split_axis=0, concat_axis=0, tiled=True
    ).reshape(n, width)
    mixed = jnp.dot(
        combine,
        back.astype(f32),
        precision=lax.Precision.HIGHEST,
        preferred_element_type=f32,
    )
    return (hstate + mixed).astype(bf16)


def solution(mesh):
    fine = Mesh(mesh.devices.reshape(NX, NZ, NC, NH, NY), CTX + EXP)
    placed = (
        P(CTX, EXP),
        P(CTX, EXP),
        P(CTX, EXP),
        P(EXP, CTX),
        P(CTX + EXP, None),
        P(),
        P(EXP, None, CTX),
        P(EXP, None, CTX),
        P(EXP, CTX, None),
        P(CTX + EXP, None),
        P(CTX + EXP, None),
    )
    return jax.shard_map(
        shards, mesh=fine, in_specs=placed, out_specs=P(CTX + EXP, None), check_vma=False
    )
```

```python
import math

import jax
import jax.numpy as jnp
from jax import lax
from jax.experimental import pallas as pl
from jax.experimental.pallas import tpu as pltpu
from jax.sharding import Mesh
from jax.sharding import PartitionSpec as P

HD = 128
EXPERTS = 8
NX, NZ, NC, NH, NY = 2, 8, 2, 2, 4
CTX = ("xl", "z", "c")
EXP = ("xh", "y")
SWAP = [(0, 1), (1, 0)]
bf16 = jnp.bfloat16
f32 = jnp.float32


HALF = NZ // 2


def even(x):
    return lax.ppermute(x, "z", [(i, i ^ 1) for i in range(NZ)])


def odd(x):
    return lax.ppermute(x, "z", [(i, (i + 1 if i % 2 else i - 1) % NZ) for i in range(NZ)])


def add(p, q):
    return (p.astype(f32) + q.astype(f32)).astype(bf16)


def ring_reduce(parts):
    half = parts[0].shape[0] // 2
    far = parts[HALF]
    ra, rb = even(far[:half]), odd(far[half:])
    for s in range(HALF - 1, 0, -1):
        pa, pb = parts[s], parts[NZ - s]
        if s == HALF - 1:
            sa = jnp.concatenate([pa[:half], add(pa[half:], rb)], axis=0)
            sb = jnp.concatenate([add(pb[:half], ra), pb[half:]], axis=0)
        else:
            sa, sb = add(pa, rb), add(pb, ra)
        ra, rb = even(sa), odd(sb)
    return parts[0], ra, rb


def experts_kernel(x_ref, g0, u0, d0, g1, u1, d1, o_ref, wg, wu, wd, sem):
    copies = []
    for p, (g, u, d) in enumerate(((g0, u0, d0), (g1, u1, d1))):
        for k, (src, dst) in enumerate(((g, wg), (u, wu), (d, wd))):
            copies.append(pltpu.make_async_copy(src, dst.at[p], sem.at[3 * p + k]))
    for copy in copies:
        copy.start()
    x = x_ref[...]
    out = None
    for p in range(2):
        copies[3 * p].wait()
        gate = jnp.dot(x, wg[p], preferred_element_type=f32)
        copies[3 * p + 1].wait()
        upper = jnp.dot(x, wu[p], preferred_element_type=f32)
        act = (gate / (1.0 + jnp.exp(-gate)) * upper).astype(bf16)
        copies[3 * p + 2].wait()
        down = jnp.dot(act, wd[p], preferred_element_type=f32)
        out = down if out is None else out + down
    o_ref[...] = out.astype(bf16)


def run_experts(x, weights):
    rows, width = x.shape
    ff = weights[0].shape[1]
    hbm = pl.BlockSpec(memory_space=pl.ANY)
    vmem = pl.BlockSpec(memory_space=pltpu.VMEM)
    return pl.pallas_call(
        experts_kernel,
        out_shape=jax.ShapeDtypeStruct((rows, width), bf16),
        in_specs=[vmem] + [hbm] * 6,
        out_specs=vmem,
        scratch_shapes=[
            pltpu.VMEM((2, width, ff), bf16),
            pltpu.VMEM((2, width, ff), bf16),
            pltpu.VMEM((2, ff, width), bf16),
            pltpu.SemaphoreType.DMA((6,)),
        ],
        compiler_params=pltpu.CompilerParams(vmem_limit_bytes=44 * 1024 * 1024),
        cost_estimate=pl.CostEstimate(
            flops=2 * 6 * rows * width * ff,
            bytes_accessed=12 * width * ff + 4 * rows * width,
            transcendentals=2 * rows * ff,
        ),
        name="experts",
    )(x, *weights)


def call(kernel, out_shape, args, smem=0, mib=24, name=None, **kw):
    vmem = pl.BlockSpec(memory_space=pltpu.VMEM)
    return pl.pallas_call(
        kernel,
        out_shape=out_shape,
        in_specs=[pl.BlockSpec(memory_space=pltpu.SMEM)] * smem + [vmem] * (len(args) - smem),
        out_specs=jax.tree.map(lambda _: vmem, out_shape),
        compiler_params=pltpu.CompilerParams(vmem_limit_bytes=mib * 1024 * 1024),
        name=name,
        **kw,
    )(*args)


def pack_kernel(k0, v0, k1, v1, o_ref):
    rows = k0.shape[0]
    o_ref[:rows, :HD] = k0[...]
    o_ref[:rows, HD:] = v0[...]
    o_ref[rows:, :HD] = k1[...]
    o_ref[rows:, HD:] = v1[...]


def attention_kernel(first, q_ref, kpos_ref, mine_ref, other_ref, o_ref):
    rows, group = q_ref.shape[0], q_ref.shape[1] // HD
    q = jnp.concatenate([q_ref[:, h * HD : (h + 1) * HD] for h in range(group)], axis=0)
    q_position = first[0] + lax.broadcasted_iota(jnp.int32, (rows, 1), 0)
    q_position = jnp.concatenate([q_position] * group, axis=0)
    scale = 1.0 / math.sqrt(HD)
    scores = []
    for i, ref in enumerate((mine_ref, other_ref)):
        s = lax.dot_general(
            q, ref[:, :HD], (((1,), (1,)), ((), ())), preferred_element_type=f32
        )
        scores.append(jnp.where(kpos_ref[i : i + 1, :] <= q_position, s * scale, -1e30))
    top = jnp.maximum(*[jnp.max(s, axis=-1, keepdims=True) for s in scores])
    total, acc = 0.0, 0.0
    for s, ref in zip(scores, (mine_ref, other_ref)):
        w = jnp.exp(s - top)
        total = total + jnp.sum(w, axis=-1, keepdims=True)
        acc = acc + jnp.dot(w.astype(bf16), ref[:, HD:], preferred_element_type=f32)
    heads = (acc / total).astype(bf16)
    for h in range(group):
        o_ref[:, h * HD : (h + 1) * HD] = heads[h * rows : (h + 1) * rows]


def project_kernel(heads_ref, mine_ref, other_ref, o_ref):
    rows = o_ref.shape[1] // 2
    for i, ref in enumerate((mine_ref, other_ref)):
        p = jnp.dot(heads_ref[...], ref[...], preferred_element_type=f32)
        for e in range(EXPERTS):
            o_ref[e, i * rows : (i + 1) * rows, :] = p[e * rows : (e + 1) * rows].astype(bf16)


def tail_kernel(src_ref, parts_ref, residual_ref, gain_ref, placing_ref, h_ref, o_ref, sum_ref):
    rows, width = h_ref.shape
    half = width // 2
    total = parts_ref[0].astype(f32)
    for e in range(1, EXPERTS):
        total = total + parts_ref[e].astype(f32)
    sum_ref[:, :half] = total[:rows]
    sum_ref[:, half:] = total[rows:]
    for j in range(width // HD):
        lanes = pl.ds(pl.multiple_of(src_ref[j] * HD, HD), HD)
        to = slice(j * HD, (j + 1) * HD)
        h_ref[:, to] = residual_ref[:, to].astype(f32) + sum_ref[:, lanes]
    h = h_ref[...]
    meansq = jnp.mean(h * h, axis=-1, keepdims=True)
    normed = (h * lax.rsqrt(meansq + 1e-05) * gain_ref[...]).astype(bf16)
    cut_rows(jnp.dot(placing_ref[...], normed, preferred_element_type=f32).astype(bf16), o_ref)


def cut_rows(x, o_ref):
    cap = x.shape[0] // EXPERTS
    cuts, piece = o_ref.shape[1] // cap, o_ref.shape[2]
    for e in range(EXPERTS):
        for i in range(cuts):
            o_ref[e, i * cap : (i + 1) * cap, :] = x[
                e * cap : (e + 1) * cap, i * piece : (i + 1) * piece
            ]


def join_rows(x_ref, cap):
    cuts = x_ref.shape[1] // cap
    return jnp.concatenate(
        [
            jnp.concatenate([x_ref[e, i * cap : (i + 1) * cap, :] for i in range(cuts)], axis=1)
            for e in range(EXPERTS)
        ],
        axis=0,
    )


def join_kernel(x_ref, o_ref):
    o_ref[...] = join_rows(x_ref, o_ref.shape[0] // EXPERTS)


def close_kernel(near_ref, a_ref, b_ref, over_ref, o_ref):
    total = near_ref[...].astype(f32) + a_ref[...].astype(f32)
    total = total + b_ref[...].astype(f32) + over_ref[...].astype(f32)
    cut_rows(total.astype(bf16), o_ref)


def mix_kernel(h_ref, combine_ref, back_ref, o_ref):
    rows = join_rows(back_ref, combine_ref.shape[1] // EXPERTS).astype(f32)
    mixed = jnp.dot(
        combine_ref[...], rows, precision=lax.Precision.HIGHEST, preferred_element_type=f32
    )
    o_ref[...] = (h_ref[...] + mixed).astype(bf16)


def shards(
    queries,
    keys,
    values,
    out_weight,
    residual,
    norm_gain,
    gate_weight,
    up_weight,
    down_weight,
    route_ids,
    route_weight,
):
    xl, z, c = lax.axis_index("xl"), lax.axis_index("z"), lax.axis_index("c")
    tok_blk = queries.shape[0]
    group = queries.shape[1] // HD
    width = residual.shape[1]
    ctx = (xl * NZ + z) * NC + c
    block_first = ctx * tok_blk

    def other_x(x):
        return lax.ppermute(x, "xl", SWAP)

    def other_core(x):
        return lax.ppermute(x, "c", SWAP)

    def ring_step(a, b, *after):
        if after:
            a, b, *_ = lax.optimization_barrier((a, b) + after)
        return even(b), odd(a)

    k_x, v_x, ow_x = other_x(keys), other_x(values), other_x(out_weight)
    pair = call(
        pack_kernel,
        jax.ShapeDtypeStruct((2 * tok_blk, 2 * HD), bf16),
        (keys, values, k_x, v_x),
        name="pack",
    )
    ow_pair = jnp.concatenate([out_weight, ow_x], axis=1)
    half, ow_half = tok_blk, out_weight.shape[0] // 2
    a1, b1 = ring_step(pair, pair)
    wa1, wb1 = ring_step(ow_pair, ow_pair)
    a2, b2 = ring_step(a1, b1)
    wa2, wb2 = ring_step(wa1, wb1)
    a3, b3 = ring_step(a2, b2)
    a4, b4 = ring_step(a3[half:], b3[:half])
    mine = jnp.concatenate([pair, a1, a2, a3, a4, b4, b3, b2, b1], axis=0)
    wa3, wb3 = ring_step(wa2, wb2, a4, b4)
    other = other_core(mine)
    wa4, wb4 = ring_step(wa3[ow_half:], wb3[:ow_half], other)
    far = jnp.concatenate([wa4, wb4], axis=0)
    ow_mine = jnp.concatenate([ow_pair, wa1, wa2, wa3, far, wb3, wb2, wb1], axis=1)
    ow_other = other_core(ow_mine)

    core_of = jnp.stack([c, 1 - c])[:, None, None, None]
    turn = 1 - 2 * (z % 2)
    z_of = ((z + turn * jnp.arange(NZ, dtype=jnp.int32)) % NZ)[None, :, None, None]
    x_of = jnp.stack([xl, 1 - xl])[None, None, :, None]
    k_position = (
        ((x_of * NZ + z_of) * NC + core_of) * tok_blk
        + jnp.arange(tok_blk, dtype=jnp.int32)[None, None, None, :]
    ).reshape(NC, -1)

    gate_o, up_o, down_o = other_core(gate_weight[0]), other_core(up_weight[0]), other_core(down_weight[0])

    heads = call(
        attention_kernel,
        jax.ShapeDtypeStruct((tok_blk, group * HD), bf16),
        (block_first[None], queries, k_position, mine, other),
        smem=1,
        name="attention",
        cost_estimate=pl.CostEstimate(
            flops=4 * tok_blk * group * HD * k_position.size,
            bytes_accessed=4 * HD * k_position.size,
            transcendentals=tok_blk * group * k_position.size,
        ),
    )
    heads, gate_o, up_o, down_o = lax.optimization_barrier((heads, gate_o, up_o, down_o))
    tok_dev = residual.shape[0]
    part = call(
        project_kernel,
        jax.ShapeDtypeStruct((EXPERTS, 2 * tok_dev, width // 2), bf16),
        (heads, ow_mine, ow_other),
        name="project",
        mib=32,
    )
    parts = lax.all_to_all(part, EXP, split_axis=0, concat_axis=0, tiled=True)
    xs = jnp.arange(NX, dtype=jnp.int32)[:, None, None]
    zs = jnp.arange(NZ, dtype=jnp.int32)[None, :, None]
    cs = jnp.arange(NC, dtype=jnp.int32)[None, None, :]
    source = (((cs ^ c) * NZ + (turn * (zs - z)) % NZ) * NX + (xs ^ xl)).reshape(-1)

    picks = route_ids.shape[1]
    cap = 2 * tok_dev * picks // EXPERTS
    flat_ids = route_ids.reshape(-1)
    onehot = (flat_ids[:, None] == jnp.arange(EXPERTS, dtype=jnp.int32)[None, :]).astype(jnp.int32)
    earlier = jnp.cumsum(onehot, axis=0) - onehot
    slot = jnp.sum(earlier * onehot, axis=1)
    place = flat_ids * cap + slot
    hits = (
        jnp.arange(EXPERTS * cap, dtype=jnp.int32)[None, :] == place[:, None]
    ).reshape(tok_dev, picks, EXPERTS * cap)
    placing = jnp.any(hits, axis=1).astype(bf16).T
    combine = jnp.sum(jnp.where(hits, route_weight[:, :, None], 0.0), axis=1)
    n = EXPERTS * cap
    cuts = 4
    cut = jax.ShapeDtypeStruct((EXPERTS, cuts * cap, width // cuts), bf16)
    hstate, outgoing = call(
        tail_kernel,
        (jax.ShapeDtypeStruct((tok_dev, width), f32), cut),
        (source, parts, residual, norm_gain[None, :], placing),
        smem=1,
        name="tail",
        scratch_shapes=[pltpu.VMEM((tok_dev, width), f32)],
    )
    rows = call(
        join_kernel,
        jax.ShapeDtypeStruct((n, width), bf16),
        (lax.all_to_all(outgoing, EXP, split_axis=0, concat_axis=0, tiled=True),),
        name="join",
    )

    panels = (gate_weight[0], up_weight[0], down_weight[0], gate_o, up_o, down_o)
    near, over = [None] * NZ, [None] * NZ
    near[0], over[0] = rows, other_x(rows)
    done_near, done_over = [None] * NZ, [None] * NZ

    def work(s):
        t = NZ - s
        if s == 0:
            out = run_experts(jnp.concatenate([near[0], over[0]], axis=0), panels)
            done_near[0], done_over[0] = out[:n], out[n:]
        else:
            out = run_experts(
                jnp.concatenate([near[s], near[t], over[s], over[t]], axis=0), panels
            )
            done_near[s], done_near[t] = out[:n], out[n : 2 * n]
            done_over[s], done_over[t] = out[2 * n : 3 * n], out[3 * n :]
        return out

    na = nb = near[0]
    oa = ob = over[0]
    for s in range(1, HALF):
        na, nb = ring_step(na, nb)
        oa, ob = ring_step(oa, ob)
        near[s], near[NZ - s] = na, nb
        over[s], over[NZ - s] = oa, ob
        out = work(s - 1)
        oa, ob, _ = lax.optimization_barrier((oa, ob, out))
        if s == HALF - 1:
            na, nb, _ = lax.optimization_barrier((na, nb, out))
    h = n // 2
    near[HALF] = ring_step(na[h:], nb[:h])
    over[HALF] = ring_step(oa[h:], ob[:h])
    out = work(HALF - 1)
    over[HALF] = lax.optimization_barrier(over[HALF] + (out,))[:2]
    done_near[HALF] = run_experts(jnp.concatenate(near[HALF], axis=0), panels)
    done_over[HALF] = run_experts(jnp.concatenate(over[HALF], axis=0), panels)
    near_0, near_a, near_b = ring_reduce(done_near)
    over_0, over_a, over_b = ring_reduce(done_over)
    sum_over = (over_0.astype(f32) + over_a.astype(f32) + over_b.astype(f32)).astype(bf16)
    mixed_rows = call(close_kernel, cut, (near_0, near_a, near_b, other_x(sum_over)), name="close")
    back = lax.all_to_all(mixed_rows, EXP, split_axis=0, concat_axis=0, tiled=True)
    return call(
        mix_kernel,
        jax.ShapeDtypeStruct((tok_dev, width), bf16),
        (hstate, combine, back),
        name="mix",
    )


def solution(mesh):
    fine = Mesh(mesh.devices.reshape(NX, NZ, NC, NH, NY), CTX + EXP)
    placed = (
        P(CTX, EXP),
        P(CTX, EXP),
        P(CTX, EXP),
        P(EXP, CTX),
        P(CTX + EXP, None),
        P(),
        P(EXP, None, CTX),
        P(EXP, None, CTX),
        P(EXP, CTX, None),
        P(CTX + EXP, None),
        P(CTX + EXP, None),
    )
    return jax.shard_map(
        shards, mesh=fine, in_specs=placed, out_specs=P(CTX + EXP, None), check_vma=False
    )
```

```python
import functools
import math

import jax
import jax.numpy as jnp
from jax import lax
from jax.experimental import pallas as pl
from jax.experimental.pallas import tpu as pltpu
from jax.sharding import Mesh
from jax.sharding import PartitionSpec as P

HD = 128
EXPERTS = 8
NX, NZ, NC, NH, NY = 2, 8, 2, 2, 4
CTX = ("xl", "z", "c")
EXP = ("xh", "y")
SEQ_BLOCKS = NX * NZ * NC
SWAP = [(0, 1), (1, 0)]
bf16 = jnp.bfloat16
f32 = jnp.float32


HALF = NZ // 2


def even(x):
    return lax.ppermute(x, "z", [(i, i ^ 1) for i in range(NZ)])


def odd(x):
    return lax.ppermute(x, "z", [(i, (i + 1 if i % 2 else i - 1) % NZ) for i in range(NZ)])


def add_kernel(first, rows, p_ref, q_ref, o_ref):
    p = p_ref[first : first + o_ref.shape[0], :]
    at, size = rows
    if size < o_ref.shape[0]:
        o_ref[...] = p
    o_ref[at : at + size, :] = (
        p[at : at + size].astype(f32) + q_ref[...].astype(f32)
    ).astype(bf16)


def add(term, rows, q, at=0):
    block, first = term
    return call(
        functools.partial(add_kernel, first, (at, q.shape[0])),
        jax.ShapeDtypeStruct((rows, q.shape[1]), bf16),
        (block, q),
        name="add",
    )


def ring_reduce(parts, rows, half, *after):
    far, at = parts[HALF]
    ra, rb = even(far[at : at + half]), odd(far[at + half : at + rows])
    for s in range(HALF - 1, 0, -1):
        last = s == HALF - 1
        sa = add(parts[s], rows, rb, half if last else 0)
        sb = add(parts[NZ - s], rows, ra)
        if after and s == 1:
            sa, sb, *_ = lax.optimization_barrier((sa, sb) + after)
        ra, rb = even(sa), odd(sb)
    return ra, rb


def experts_kernel(x_ref, g0, u0, d0, g1, u1, d1, o_ref, wg, wu, wd, sem):
    copies = []
    for p, (g, u, d) in enumerate(((g0, u0, d0), (g1, u1, d1))):
        for k, (src, dst) in enumerate(((g, wg), (u, wu), (d, wd))):
            copies.append(pltpu.make_async_copy(src, dst.at[p], sem.at[3 * p + k]))
    for copy in copies:
        copy.start()
    x = x_ref[...]
    out = None
    for p in range(2):
        copies[3 * p].wait()
        gate = jnp.dot(x, wg[p], preferred_element_type=f32)
        copies[3 * p + 1].wait()
        upper = jnp.dot(x, wu[p], preferred_element_type=f32)
        act = (gate / (1.0 + jnp.exp(-gate)) * upper).astype(bf16)
        copies[3 * p + 2].wait()
        down = jnp.dot(act, wd[p], preferred_element_type=f32)
        out = down if out is None else out + down
    o_ref[...] = out.astype(bf16)


def run_experts(x, weights):
    rows, width = x.shape
    ff = weights[0].shape[1]
    hbm = pl.BlockSpec(memory_space=pl.ANY)
    vmem = pl.BlockSpec(memory_space=pltpu.VMEM)
    return pl.pallas_call(
        experts_kernel,
        out_shape=jax.ShapeDtypeStruct((rows, width), bf16),
        in_specs=[vmem] + [hbm] * 6,
        out_specs=vmem,
        scratch_shapes=[
            pltpu.VMEM((2, width, ff), bf16),
            pltpu.VMEM((2, width, ff), bf16),
            pltpu.VMEM((2, ff, width), bf16),
            pltpu.SemaphoreType.DMA((6,)),
        ],
        compiler_params=pltpu.CompilerParams(vmem_limit_bytes=40 * 1024 * 1024),
        cost_estimate=pl.CostEstimate(
            flops=2 * 6 * rows * width * ff,
            bytes_accessed=12 * width * ff + 4 * rows * width,
            transcendentals=2 * rows * ff,
        ),
        name="experts",
    )(x, *weights)


def call(kernel, out_shape, args, smem=0, mib=24, name=None, **kw):
    vmem = pl.BlockSpec(memory_space=pltpu.VMEM)
    return pl.pallas_call(
        kernel,
        out_shape=out_shape,
        in_specs=[pl.BlockSpec(memory_space=pltpu.SMEM)] * smem + [vmem] * (len(args) - smem),
        out_specs=jax.tree.map(lambda _: vmem, out_shape),
        compiler_params=pltpu.CompilerParams(vmem_limit_bytes=mib * 1024 * 1024),
        name=name,
        **kw,
    )(*args)


def pack_kernel(k0, v0, w0, k1, v1, w1, o_ref, sem):
    rows, deep = k0.shape[0], w0.shape[0]
    copies = []
    for i, ref in enumerate((k0, v0, k1, v1, w0, w1)):
        r, c = divmod(i, 2)
        first, size = (r * rows, rows) if r < 2 else (2 * rows, deep)
        to = o_ref.at[first : first + size, c * HD : (c + 1) * HD]
        copies.append(pltpu.make_async_copy(ref, to, sem.at[i]))
    for copy in copies:
        copy.start()
    for copy in copies:
        copy.wait()


def attend_kernel(first, starts, q_ref, *refs):
    cores = len(refs) - 8
    blocks, (o_hbm, k_all, v_all, w_all, o_ref, sem_k, sem_w, sem_o) = refs[:cores], refs[cores:]
    rows, group = q_ref.shape[0], q_ref.shape[1] // HD
    deep, wide = w_all.shape[2], w_all.shape[3]
    pair = 2 * rows
    waits_k, waits_w = [], []
    for i, ref in enumerate(blocks):
        core, r = divmod(i, NZ + 1)
        at = min(r, HALF) if r <= HALF else r - 1
        low = r == HALF + 1
        if not low:
            to = slice((core * NZ + at) * pair, (core * NZ + at + 1) * pair)
            waits_k.append(
                pltpu.make_async_copy(ref.at[:pair, :HD], k_all.at[to, :], sem_k.at[len(waits_k)])
            )
            waits_k.append(
                pltpu.make_async_copy(ref.at[:pair, HD:], v_all.at[to, :], sem_k.at[len(waits_k)])
            )
        skip = 0 if low else pair
        size = ref.shape[0] - skip
        begin = deep - size if low else 0
        waits_w.append(
            pltpu.make_async_copy(
                ref.at[skip:, :], w_all.at[core, at, begin : begin + size, :], sem_w.at[i]
            )
        )
    for copy in waits_k + waits_w:
        copy.start()
    q = jnp.concatenate([q_ref[:, h * HD : (h + 1) * HD] for h in range(group)], axis=0)
    q_position = first[0] + lax.broadcasted_iota(jnp.int32, (rows, 1), 0)
    q_position = jnp.concatenate([q_position] * group, axis=0)
    scale = 1.0 / math.sqrt(HD)
    for copy in waits_k:
        copy.wait()
    part = NZ * pair
    column = lax.broadcasted_iota(jnp.int32, (1, part), 1)
    scores = []
    for core in range(NC):
        s = lax.dot_general(
            q,
            k_all[core * part : (core + 1) * part, :],
            (((1,), (1,)), ((), ())),
            preferred_element_type=f32,
        )
        shift = jnp.zeros((1, part), jnp.int32)
        for j in range(2 * NZ):
            shift = jnp.where(column >= j * rows, starts[core * 2 * NZ + j] - j * rows, shift)
        scores.append(jnp.where(column + shift <= q_position, s * scale, -1e30))
    top = jnp.maximum(*[jnp.max(s, axis=-1, keepdims=True) for s in scores])
    total, acc = 0.0, 0.0
    for core, s in enumerate(scores):
        w = jnp.exp(s - top)
        total = total + jnp.sum(w, axis=-1, keepdims=True)
        acc = acc + jnp.dot(
            w.astype(bf16),
            v_all[core * part : (core + 1) * part, :],
            preferred_element_type=f32,
        )
    heads = (acc / total).astype(bf16)
    heads = jnp.concatenate([heads[h * rows : (h + 1) * rows] for h in range(group)], axis=1)
    for copy in waits_w:
        copy.wait()
    tok = rows // EXPERTS
    out = []
    for r in range(NZ):
        p = [
            jnp.dot(heads, w_all[core, r], preferred_element_type=f32) for core in range(NC)
        ]
        for e in range(EXPERTS):
            both = jnp.concatenate([x[e * tok : (e + 1) * tok] for x in p], axis=0)
            o_ref[e, :, r * wide : (r + 1) * wide] = both.astype(bf16)
        to = slice(r * wide, (r + 1) * wide)
        copy = pltpu.make_async_copy(o_ref.at[:, :, to], o_hbm.at[:, :, to], sem_o.at[r])
        copy.start()
        out.append(copy)
    for copy in out:
        copy.wait()


def tail_kernel(src_ref, parts_ref, residual_ref, gain_ref, placing_ref, h_ref, o_ref, sum_ref):
    rows, width = h_ref.shape
    half = width // 2
    total = parts_ref[0].astype(f32)
    for e in range(1, EXPERTS):
        total = total + parts_ref[e].astype(f32)
    sum_ref[:, :half] = total[:rows]
    sum_ref[:, half:] = total[rows:]
    for j in range(width // HD):
        lanes = pl.ds(pl.multiple_of(src_ref[j] * HD, HD), HD)
        to = slice(j * HD, (j + 1) * HD)
        h_ref[:, to] = residual_ref[:, to].astype(f32) + sum_ref[:, lanes]
    h = h_ref[...]
    meansq = jnp.mean(h * h, axis=-1, keepdims=True)
    normed = (h * lax.rsqrt(meansq + 1e-05) * gain_ref[...]).astype(bf16)
    cut_rows(jnp.dot(placing_ref[...], normed, preferred_element_type=f32), o_ref)


def cut_rows(x, o_ref):
    cap = x.shape[0] // EXPERTS
    cuts, piece = o_ref.shape[1] // cap, o_ref.shape[2]
    for e in range(EXPERTS):
        rows = x[e * cap : (e + 1) * cap]
        o_ref[e] = jnp.concatenate(
            [rows[:, i * piece : (i + 1) * piece] for i in range(cuts)], axis=0
        ).astype(bf16)


def join_rows(x_ref, cap):
    cuts = x_ref.shape[1] // cap
    blocks = [x_ref[e].astype(f32) for e in range(EXPERTS)]
    return jnp.concatenate(
        [
            jnp.concatenate([x[i * cap : (i + 1) * cap] for i in range(cuts)], axis=1)
            for x in blocks
        ],
        axis=0,
    )


def join_kernel(x_ref, o_ref):
    o_ref[...] = join_rows(x_ref, o_ref.shape[0] // EXPERTS).astype(bf16)


def close_kernel(xl, own_ref, na, nb, oa, ob, o_ref):
    n = na.shape[0]
    for i, (a, b) in enumerate(((na, nb), (oa, ob))):
        total = own_ref[i * n : (i + 1) * n, :].astype(f32) + a[...].astype(f32)
        total = total + b[...].astype(f32)
        cut_rows(total, o_ref.at[xl[0] if i == 0 else 1 - xl[0]])


def mix_kernel(h_ref, combine_ref, back_ref, o_ref):
    cap = combine_ref.shape[1] // EXPERTS
    rows = join_rows(back_ref.at[0], cap) + join_rows(back_ref.at[1], cap)
    mixed = jnp.dot(
        combine_ref[...], rows, precision=lax.Precision.HIGHEST, preferred_element_type=f32
    )
    o_ref[...] = (h_ref[...] + mixed).astype(bf16)


def shards(
    queries,
    keys,
    values,
    out_weight,
    residual,
    norm_gain,
    gate_weight,
    up_weight,
    down_weight,
    route_ids,
    route_weight,
):
    xl, z, c = lax.axis_index("xl"), lax.axis_index("z"), lax.axis_index("c")
    tok_blk = queries.shape[0]
    group = queries.shape[1] // HD
    width = residual.shape[1]
    ctx = (xl * NZ + z) * NC + c
    block_first = ctx * tok_blk

    def other_x(x):
        return lax.ppermute(x, "xl", SWAP)

    def other_core(x):
        return lax.ppermute(x, "c", SWAP)

    def ring_step(a, b, *after):
        if after:
            a, b, *_ = lax.optimization_barrier((a, b) + after)
        return even(b), odd(a)

    theirs = other_x(keys), other_x(values), other_x(out_weight)
    own = pl.pallas_call(
        pack_kernel,
        out_shape=jax.ShapeDtypeStruct((2 * tok_blk + out_weight.shape[0], 2 * HD), bf16),
        in_specs=[pl.BlockSpec(memory_space=pl.ANY)] * 6,
        out_specs=pl.BlockSpec(memory_space=pltpu.VMEM),
        compiler_params=pltpu.CompilerParams(vmem_limit_bytes=4 * 1024 * 1024),
        scratch_shapes=[pltpu.SemaphoreType.DMA((6,))],
        name="pack",
    )(keys, values, out_weight, *theirs)
    half = own.shape[0] // 2
    came = [own] + [None] * (NZ - 1)
    a = b = own
    for s in range(1, HALF):
        a, b = ring_step(a, b)
        came[s], came[NZ - s] = a, b
    came[HALF : HALF + 1] = ring_step(a[half:], b[:half])
    came = came + [other_core(x) for x in came]

    core_of = jnp.stack([c, 1 - c])[:, None, None]
    turn = 1 - 2 * (z % 2)
    z_of = ((z + turn * jnp.arange(NZ, dtype=jnp.int32)) % NZ)[None, :, None]
    x_of = jnp.stack([xl, 1 - xl])[None, None, :]
    starts = (((x_of * NZ + z_of) * NC + core_of) * tok_blk).reshape(-1)
    keys_all = SEQ_BLOCKS * tok_blk
    tok_dev = residual.shape[0]
    deep = out_weight.shape[0]
    hbm = pl.BlockSpec(memory_space=pl.ANY)
    smem = pl.BlockSpec(memory_space=pltpu.SMEM)
    part_shape = (EXPERTS, 2 * tok_dev, width // 2)
    part = pl.pallas_call(
        attend_kernel,
        out_shape=jax.ShapeDtypeStruct(part_shape, bf16),
        in_specs=[smem, smem, pl.BlockSpec(memory_space=pltpu.VMEM)] + [hbm] * len(came),
        out_specs=hbm,
        scratch_shapes=[
            pltpu.VMEM((keys_all, HD), bf16),
            pltpu.VMEM((keys_all, HD), bf16),
            pltpu.VMEM((NC, NZ, deep, 2 * HD), bf16),
            pltpu.VMEM(part_shape, bf16),
            pltpu.SemaphoreType.DMA((4 * NZ,)),
            pltpu.SemaphoreType.DMA((len(came),)),
            pltpu.SemaphoreType.DMA((NZ,)),
        ],
        compiler_params=pltpu.CompilerParams(vmem_limit_bytes=60 * 1024 * 1024),
        cost_estimate=pl.CostEstimate(
            flops=4 * tok_blk * group * HD * keys_all + 2 * tok_blk * deep * width,
            bytes_accessed=4 * HD * keys_all + 2 * deep * width,
            transcendentals=tok_blk * group * keys_all,
        ),
        name="attend",
    )(block_first[None], starts, queries, *came)
    panels = lax.optimization_barrier((gate_weight[0], up_weight[0], down_weight[0], part))
    part = panels[3]
    panels_o = tuple(other_core(x) for x in panels[:3])
    parts = lax.all_to_all(part, EXP, split_axis=0, concat_axis=0, tiled=True)
    parts, *panels_o = lax.optimization_barrier((parts,) + panels_o)
    xs = jnp.arange(NX, dtype=jnp.int32)[:, None, None]
    zs = jnp.arange(NZ, dtype=jnp.int32)[None, :, None]
    cs = jnp.arange(NC, dtype=jnp.int32)[None, None, :]
    source = (((cs ^ c) * NZ + (turn * (zs - z)) % NZ) * NX + (xs ^ xl)).reshape(-1)

    picks = route_ids.shape[1]
    cap = 2 * tok_dev * picks // EXPERTS
    flat_ids = route_ids.reshape(-1)
    onehot = (flat_ids[:, None] == jnp.arange(EXPERTS, dtype=jnp.int32)[None, :]).astype(jnp.int32)
    earlier = jnp.cumsum(onehot, axis=0) - onehot
    slot = jnp.sum(earlier * onehot, axis=1)
    place = flat_ids * cap + slot
    hits = (
        jnp.arange(EXPERTS * cap, dtype=jnp.int32)[None, :] == place[:, None]
    ).reshape(tok_dev, picks, EXPERTS * cap)
    placing = jnp.any(hits, axis=1).astype(bf16).T
    combine = jnp.sum(jnp.where(hits, route_weight[:, :, None], 0.0), axis=1)
    n = EXPERTS * cap
    cuts = 4
    cut = jax.ShapeDtypeStruct((EXPERTS, cuts * cap, width // cuts), bf16)
    hstate, outgoing = call(
        tail_kernel,
        (jax.ShapeDtypeStruct((tok_dev, width), f32), cut),
        (source, parts, residual, norm_gain[None, :], placing),
        smem=1,
        name="tail",
        scratch_shapes=[pltpu.VMEM((tok_dev, width), f32)],
    )
    rows = call(
        join_kernel,
        jax.ShapeDtypeStruct((n, width), bf16),
        (lax.all_to_all(outgoing, EXP, split_axis=0, concat_axis=0, tiled=True),),
        name="join",
    )

    panels = (gate_weight[0], up_weight[0], down_weight[0], *panels_o)
    near, over = [None] * NZ, [None] * NZ
    near[0], over[0] = rows, other_x(rows)
    done_near, done_over = [None] * NZ, [None] * NZ

    def work(*steps):
        blocks = []
        for s in steps:
            if s == HALF:
                pieces = [near[s], over[s]]
            else:
                pieces = [(near[s],), (near[NZ - s],), (over[s],), (over[NZ - s],)]
            blocks += [x for piece in pieces for x in piece]
        out = run_experts(jnp.concatenate(blocks, axis=0), panels)
        at = 0
        for s in steps:
            if s == HALF:
                done_near[s], done_over[s] = (out, at), (out, at + n)
                at += 2 * n
            else:
                done_near[s], done_near[NZ - s] = (out, at), (out, at + n)
                done_over[s], done_over[NZ - s] = (out, at + 2 * n), (out, at + 3 * n)
                at += 4 * n
        return out

    own = run_experts(jnp.concatenate([near[0], over[0]], axis=0), panels)
    na = nb = near[0]
    oa = ob = over[0]
    for s in range(1, HALF):
        na, nb = ring_step(na, nb)
        oa, ob = ring_step(oa, ob)
        near[s], near[NZ - s] = na, nb
        over[s], over[NZ - s] = oa, ob
    na, nb, _ = lax.optimization_barrier((na, nb, work(1, 2)))
    near_half, over_half = n // 3, n - n // 3
    near[HALF] = ring_step(na[near_half:], nb[:near_half])
    over[HALF] = ring_step(oa[over_half:], ob[:over_half])
    work(3, HALF)
    sums_near = ring_reduce(done_near, n, near_half, own)
    sums_over = ring_reduce(done_over, n, over_half)
    ready = call(
        close_kernel,
        jax.ShapeDtypeStruct((NX,) + cut.shape, bf16),
        (xl[None], own) + sums_near + sums_over,
        smem=1,
        name="close",
    )
    back = lax.all_to_all(
        ready.reshape((NX * EXPERTS,) + cut.shape[1:]),
        ("xl",) + EXP,
        split_axis=0,
        concat_axis=0,
        tiled=True,
    ).reshape(ready.shape)
    return call(
        mix_kernel,
        jax.ShapeDtypeStruct((tok_dev, width), bf16),
        (hstate, combine, back),
        name="mix",
    )


def solution(mesh):
    fine = Mesh(mesh.devices.reshape(NX, NZ, NC, NH, NY), CTX + EXP)
    placed = (
        P(CTX, EXP),
        P(CTX, EXP),
        P(CTX, EXP),
        P(EXP, CTX),
        P(CTX + EXP, None),
        P(),
        P(EXP, None, CTX),
        P(EXP, None, CTX),
        P(EXP, CTX, None),
        P(CTX + EXP, None),
        P(CTX + EXP, None),
    )
    return jax.shard_map(
        shards, mesh=fine, in_specs=placed, out_specs=P(CTX + EXP, None), check_vma=False
    )
```

```python
import functools
import math

import jax
import jax.numpy as jnp
from jax import lax
from jax.experimental import pallas as pl
from jax.experimental.pallas import tpu as pltpu
from jax.sharding import Mesh
from jax.sharding import PartitionSpec as P

HD = 128
EXPERTS = 8
NX, NZ, NC, NH, NY = 2, 8, 2, 2, 4
CTX = ("xl", "z", "c")
EXP = ("xh", "y")
SEQ_BLOCKS = NX * NZ * NC
SWAP = [(0, 1), (1, 0)]
bf16 = jnp.bfloat16
f32 = jnp.float32


HALF = NZ // 2
PLAN = [('o2', (0,)), ('o3', (1,)), ('n4', (2,))]
LAST = (3, 4)
OWN_LAST = False


def even(x):
    return lax.ppermute(x, "z", [(i, i ^ 1) for i in range(NZ)])


def odd(x):
    return lax.ppermute(x, "z", [(i, (i + 1 if i % 2 else i - 1) % NZ) for i in range(NZ)])


def add_kernel(first, rows, p_ref, q_ref, o_ref):
    p = p_ref[first : first + o_ref.shape[0], :]
    at, size = rows
    if size < o_ref.shape[0]:
        o_ref[...] = p
    o_ref[at : at + size, :] = (
        p[at : at + size].astype(f32) + q_ref[...].astype(f32)
    ).astype(bf16)


def add(term, rows, q, at=0):
    block, first = term
    return call(
        functools.partial(add_kernel, first, (at, q.shape[0])),
        jax.ShapeDtypeStruct((rows, q.shape[1]), bf16),
        (block, q),
        name="add",
    )


def ring_reduce(parts, rows, half, *after):
    far, at = parts[HALF]
    ra, rb = even(far[at : at + half]), odd(far[at + half : at + rows])
    for s in range(HALF - 1, 0, -1):
        last = s == HALF - 1
        sa = add(parts[s], rows, rb, half if last else 0)
        sb = add(parts[NZ - s], rows, ra)
        if after and s == 1:
            sa, sb, *_ = lax.optimization_barrier((sa, sb) + after)
        ra, rb = even(sa), odd(sb)
    return ra, rb


def experts_kernel(x_ref, g0, u0, d0, g1, u1, d1, o_ref, wg, wu, wd, sem):
    copies = []
    for p, (g, u, d) in enumerate(((g0, u0, d0), (g1, u1, d1))):
        for k, (src, dst) in enumerate(((g, wg), (u, wu), (d, wd))):
            copies.append(pltpu.make_async_copy(src, dst.at[p], sem.at[3 * p + k]))
    for copy in copies:
        copy.start()
    x = x_ref[...]
    out = None
    for p in range(2):
        copies[3 * p].wait()
        gate = jnp.dot(x, wg[p], preferred_element_type=f32)
        copies[3 * p + 1].wait()
        upper = jnp.dot(x, wu[p], preferred_element_type=f32)
        act = (gate / (1.0 + jnp.exp(-gate)) * upper).astype(bf16)
        copies[3 * p + 2].wait()
        down = jnp.dot(act, wd[p], preferred_element_type=f32)
        out = down if out is None else out + down
    o_ref[...] = out.astype(bf16)


def run_experts(x, weights):
    rows, width = x.shape
    ff = weights[0].shape[1]
    hbm = pl.BlockSpec(memory_space=pl.ANY)
    vmem = pl.BlockSpec(memory_space=pltpu.VMEM)
    return pl.pallas_call(
        experts_kernel,
        out_shape=jax.ShapeDtypeStruct((rows, width), bf16),
        in_specs=[vmem] + [hbm] * 6,
        out_specs=vmem,
        scratch_shapes=[
            pltpu.VMEM((2, width, ff), bf16),
            pltpu.VMEM((2, width, ff), bf16),
            pltpu.VMEM((2, ff, width), bf16),
            pltpu.SemaphoreType.DMA((6,)),
        ],
        compiler_params=pltpu.CompilerParams(vmem_limit_bytes=40 * 1024 * 1024),
        cost_estimate=pl.CostEstimate(
            flops=2 * 6 * rows * width * ff,
            bytes_accessed=12 * width * ff + 4 * rows * width,
            transcendentals=2 * rows * ff,
        ),
        name="experts",
    )(x, *weights)


def call(kernel, out_shape, args, smem=0, mib=24, name=None, **kw):
    vmem = pl.BlockSpec(memory_space=pltpu.VMEM)
    return pl.pallas_call(
        kernel,
        out_shape=out_shape,
        in_specs=[pl.BlockSpec(memory_space=pltpu.SMEM)] * smem + [vmem] * (len(args) - smem),
        out_specs=jax.tree.map(lambda _: vmem, out_shape),
        compiler_params=pltpu.CompilerParams(vmem_limit_bytes=mib * 1024 * 1024),
        name=name,
        **kw,
    )(*args)


def pack_kernel(k0, v0, w0, k1, v1, w1, o_ref, sem):
    rows, deep = k0.shape[0], w0.shape[0]
    copies = []
    for i, ref in enumerate((k0, v0, k1, v1, w0, w1)):
        r, c = divmod(i, 2)
        first, size = (r * rows, rows) if r < 2 else (2 * rows, deep)
        to = o_ref.at[first : first + size, c * HD : (c + 1) * HD]
        copies.append(pltpu.make_async_copy(ref, to, sem.at[i]))
    for copy in copies:
        copy.start()
    for copy in copies:
        copy.wait()


def attend_kernel(first, starts, q_ref, *refs):
    cores = len(refs) - 8
    blocks, (o_hbm, k_all, v_all, w_all, o_ref, sem_k, sem_w, sem_o) = refs[:cores], refs[cores:]
    rows, group = q_ref.shape[0], q_ref.shape[1] // HD
    deep, wide = w_all.shape[2], w_all.shape[3]
    pair = 2 * rows
    waits_k, waits_w = [], []
    for i, ref in enumerate(blocks):
        core, r = divmod(i, NZ + 1)
        at = min(r, HALF) if r <= HALF else r - 1
        low = r == HALF + 1
        if not low:
            to = slice((core * NZ + at) * pair, (core * NZ + at + 1) * pair)
            waits_k.append(
                pltpu.make_async_copy(ref.at[:pair, :HD], k_all.at[to, :], sem_k.at[len(waits_k)])
            )
            waits_k.append(
                pltpu.make_async_copy(ref.at[:pair, HD:], v_all.at[to, :], sem_k.at[len(waits_k)])
            )
        skip = 0 if low else pair
        size = ref.shape[0] - skip
        begin = deep - size if low else 0
        waits_w.append(
            pltpu.make_async_copy(
                ref.at[skip:, :], w_all.at[core, at, begin : begin + size, :], sem_w.at[i]
            )
        )
    for copy in waits_k + waits_w:
        copy.start()
    q = jnp.concatenate([q_ref[:, h * HD : (h + 1) * HD] for h in range(group)], axis=0)
    q_position = first[0] + lax.broadcasted_iota(jnp.int32, (rows, 1), 0)
    q_position = jnp.concatenate([q_position] * group, axis=0)
    scale = 1.0 / math.sqrt(HD)
    for copy in waits_k:
        copy.wait()
    part = NZ * pair
    column = lax.broadcasted_iota(jnp.int32, (1, part), 1)
    scores = []
    for core in range(NC):
        s = lax.dot_general(
            q,
            k_all[core * part : (core + 1) * part, :],
            (((1,), (1,)), ((), ())),
            preferred_element_type=f32,
        )
        shift = jnp.zeros((1, part), jnp.int32)
        for j in range(2 * NZ):
            shift = jnp.where(column >= j * rows, starts[core * 2 * NZ + j] - j * rows, shift)
        scores.append(jnp.where(column + shift <= q_position, s * scale, -1e30))
    top = jnp.maximum(*[jnp.max(s, axis=-1, keepdims=True) for s in scores])
    total, acc = 0.0, 0.0
    for core, s in enumerate(scores):
        w = jnp.exp(s - top)
        total = total + jnp.sum(w, axis=-1, keepdims=True)
        acc = acc + jnp.dot(
            w.astype(bf16),
            v_all[core * part : (core + 1) * part, :],
            preferred_element_type=f32,
        )
    heads = (acc / total).astype(bf16)
    heads = jnp.concatenate([heads[h * rows : (h + 1) * rows] for h in range(group)], axis=1)
    for copy in waits_w:
        copy.wait()
    tok = rows // EXPERTS
    out = []
    for r in range(NZ):
        p = [
            jnp.dot(heads, w_all[core, r], preferred_element_type=f32) for core in range(NC)
        ]
        for e in range(EXPERTS):
            both = jnp.concatenate([x[e * tok : (e + 1) * tok] for x in p], axis=0)
            o_ref[e, :, r * wide : (r + 1) * wide] = both.astype(bf16)
        to = slice(r * wide, (r + 1) * wide)
        copy = pltpu.make_async_copy(o_ref.at[:, :, to], o_hbm.at[:, :, to], sem_o.at[r])
        copy.start()
        out.append(copy)
    for copy in out:
        copy.wait()


def tail_kernel(src_ref, parts_ref, residual_ref, gain_ref, placing_ref, h_ref, o_ref, sum_ref):
    rows, width = h_ref.shape
    half = width // 2
    total = parts_ref[0].astype(f32)
    for e in range(1, EXPERTS):
        total = total + parts_ref[e].astype(f32)
    sum_ref[:, :half] = total[:rows]
    sum_ref[:, half:] = total[rows:]
    for j in range(width // HD):
        lanes = pl.ds(pl.multiple_of(src_ref[j] * HD, HD), HD)
        to = slice(j * HD, (j + 1) * HD)
        h_ref[:, to] = residual_ref[:, to].astype(f32) + sum_ref[:, lanes]
    h = h_ref[...]
    meansq = jnp.mean(h * h, axis=-1, keepdims=True)
    normed = (h * lax.rsqrt(meansq + 1e-05) * gain_ref[...]).astype(bf16)
    cut_rows(jnp.dot(placing_ref[...], normed, preferred_element_type=f32), o_ref)


def cut_rows(x, o_ref):
    cap = x.shape[0] // EXPERTS
    cuts, piece = o_ref.shape[1] // cap, o_ref.shape[2]
    for e in range(EXPERTS):
        rows = x[e * cap : (e + 1) * cap]
        o_ref[e] = jnp.concatenate(
            [rows[:, i * piece : (i + 1) * piece] for i in range(cuts)], axis=0
        ).astype(bf16)


def join_rows(x_ref, cap):
    cuts = x_ref.shape[1] // cap
    blocks = [x_ref[e].astype(f32) for e in range(EXPERTS)]
    return jnp.concatenate(
        [
            jnp.concatenate([x[i * cap : (i + 1) * cap] for i in range(cuts)], axis=1)
            for x in blocks
        ],
        axis=0,
    )


def join_kernel(x_ref, o_ref):
    o_ref[...] = join_rows(x_ref, o_ref.shape[0] // EXPERTS).astype(bf16)


def close_kernel(xl, own_ref, na, nb, oa, ob, o_ref):
    n = na.shape[0]
    for i, (a, b) in enumerate(((na, nb), (oa, ob))):
        total = own_ref[i * n : (i + 1) * n, :].astype(f32) + a[...].astype(f32)
        total = total + b[...].astype(f32)
        cut_rows(total, o_ref.at[xl[0] if i == 0 else 1 - xl[0]])


def mix_kernel(h_ref, combine_ref, back_ref, o_ref):
    cap = combine_ref.shape[1] // EXPERTS
    rows = join_rows(back_ref.at[0], cap) + join_rows(back_ref.at[1], cap)
    mixed = jnp.dot(
        combine_ref[...], rows, precision=lax.Precision.HIGHEST, preferred_element_type=f32
    )
    o_ref[...] = (h_ref[...] + mixed).astype(bf16)


def shards(
    queries,
    keys,
    values,
    out_weight,
    residual,
    norm_gain,
    gate_weight,
    up_weight,
    down_weight,
    route_ids,
    route_weight,
):
    xl, z, c = lax.axis_index("xl"), lax.axis_index("z"), lax.axis_index("c")
    tok_blk = queries.shape[0]
    group = queries.shape[1] // HD
    width = residual.shape[1]
    ctx = (xl * NZ + z) * NC + c
    block_first = ctx * tok_blk

    def other_x(x):
        return lax.ppermute(x, "xl", SWAP)

    def other_core(x):
        return lax.ppermute(x, "c", SWAP)

    def ring_step(a, b, *after):
        if after:
            a, b, *_ = lax.optimization_barrier((a, b) + after)
        return even(b), odd(a)

    theirs = other_x(keys), other_x(values), other_x(out_weight)
    own = pl.pallas_call(
        pack_kernel,
        out_shape=jax.ShapeDtypeStruct((2 * tok_blk + out_weight.shape[0], 2 * HD), bf16),
        in_specs=[pl.BlockSpec(memory_space=pl.ANY)] * 6,
        out_specs=pl.BlockSpec(memory_space=pltpu.VMEM),
        compiler_params=pltpu.CompilerParams(vmem_limit_bytes=4 * 1024 * 1024),
        scratch_shapes=[pltpu.SemaphoreType.DMA((6,))],
        name="pack",
    )(keys, values, out_weight, *theirs)
    half = own.shape[0] // 2
    came = [own] + [None] * (NZ - 1)
    a = b = own
    for s in range(1, HALF):
        a, b = ring_step(a, b)
        came[s], came[NZ - s] = a, b
    came[HALF : HALF + 1] = ring_step(a[half:], b[:half])
    came = came + [other_core(x) for x in came]

    core_of = jnp.stack([c, 1 - c])[:, None, None]
    turn = 1 - 2 * (z % 2)
    z_of = ((z + turn * jnp.arange(NZ, dtype=jnp.int32)) % NZ)[None, :, None]
    x_of = jnp.stack([xl, 1 - xl])[None, None, :]
    starts = (((x_of * NZ + z_of) * NC + core_of) * tok_blk).reshape(-1)
    keys_all = SEQ_BLOCKS * tok_blk
    tok_dev = residual.shape[0]
    deep = out_weight.shape[0]
    hbm = pl.BlockSpec(memory_space=pl.ANY)
    smem = pl.BlockSpec(memory_space=pltpu.SMEM)
    part_shape = (EXPERTS, 2 * tok_dev, width // 2)
    part = pl.pallas_call(
        attend_kernel,
        out_shape=jax.ShapeDtypeStruct(part_shape, bf16),
        in_specs=[smem, smem, pl.BlockSpec(memory_space=pltpu.VMEM)] + [hbm] * len(came),
        out_specs=hbm,
        scratch_shapes=[
            pltpu.VMEM((keys_all, HD), bf16),
            pltpu.VMEM((keys_all, HD), bf16),
            pltpu.VMEM((NC, NZ, deep, 2 * HD), bf16),
            pltpu.VMEM(part_shape, bf16),
            pltpu.SemaphoreType.DMA((4 * NZ,)),
            pltpu.SemaphoreType.DMA((len(came),)),
            pltpu.SemaphoreType.DMA((NZ,)),
        ],
        compiler_params=pltpu.CompilerParams(vmem_limit_bytes=60 * 1024 * 1024),
        cost_estimate=pl.CostEstimate(
            flops=4 * tok_blk * group * HD * keys_all + 2 * tok_blk * deep * width,
            bytes_accessed=4 * HD * keys_all + 2 * deep * width,
            transcendentals=tok_blk * group * keys_all,
        ),
        name="attend",
    )(block_first[None], starts, queries, *came)
    panels = lax.optimization_barrier((gate_weight[0], up_weight[0], down_weight[0], part))
    part = panels[3]
    panels_o = tuple(other_core(x) for x in panels[:3])
    parts = lax.all_to_all(part, EXP, split_axis=0, concat_axis=0, tiled=True)
    parts, *panels_o = lax.optimization_barrier((parts,) + panels_o)
    xs = jnp.arange(NX, dtype=jnp.int32)[:, None, None]
    zs = jnp.arange(NZ, dtype=jnp.int32)[None, :, None]
    cs = jnp.arange(NC, dtype=jnp.int32)[None, None, :]
    source = (((cs ^ c) * NZ + (turn * (zs - z)) % NZ) * NX + (xs ^ xl)).reshape(-1)

    picks = route_ids.shape[1]
    cap = 2 * tok_dev * picks // EXPERTS
    flat_ids = route_ids.reshape(-1)
    onehot = (flat_ids[:, None] == jnp.arange(EXPERTS, dtype=jnp.int32)[None, :]).astype(jnp.int32)
    earlier = jnp.cumsum(onehot, axis=0) - onehot
    slot = jnp.sum(earlier * onehot, axis=1)
    place = flat_ids * cap + slot
    hits = (
        jnp.arange(EXPERTS * cap, dtype=jnp.int32)[None, :] == place[:, None]
    ).reshape(tok_dev, picks, EXPERTS * cap)
    placing = jnp.any(hits, axis=1).astype(bf16).T
    combine = jnp.sum(jnp.where(hits, route_weight[:, :, None], 0.0), axis=1)
    n = EXPERTS * cap
    cuts = 4
    cut = jax.ShapeDtypeStruct((EXPERTS, cuts * cap, width // cuts), bf16)
    hstate, outgoing = call(
        tail_kernel,
        (jax.ShapeDtypeStruct((tok_dev, width), f32), cut),
        (source, parts, residual, norm_gain[None, :], placing),
        smem=1,
        name="tail",
        scratch_shapes=[pltpu.VMEM((tok_dev, width), f32)],
    )
    rows = call(
        join_kernel,
        jax.ShapeDtypeStruct((n, width), bf16),
        (lax.all_to_all(outgoing, EXP, split_axis=0, concat_axis=0, tiled=True),),
        name="join",
    )

    panels = (gate_weight[0], up_weight[0], down_weight[0], *panels_o)
    near, over = [None] * NZ, [None] * NZ
    near[0], over[0] = rows, other_x(rows)
    done_near, done_over = {}, {}

    def work(*steps):
        blocks = []
        for s in steps:
            if s == 0:
                pieces = [(near[0],), (over[0],)]
            elif s == HALF:
                pieces = [near[s], over[s]]
            else:
                pieces = [(near[s],), (near[NZ - s],), (over[s],), (over[NZ - s],)]
            blocks += [x for piece in pieces for x in piece]
        out = run_experts(jnp.concatenate(blocks, axis=0), panels)
        at = 0
        for s in steps:
            if s in (0, HALF):
                done_near[s], done_over[s] = (out, at), (out, at + n)
                at += 2 * n
            else:
                done_near[s], done_near[NZ - s] = (out, at), (out, at + n)
                done_over[s], done_over[NZ - s] = (out, at + 2 * n), (out, at + 3 * n)
                at += 4 * n
        return out

    na = nb = near[0]
    oa = ob = over[0]
    outs = []

    def ties(place, x, y):
        for where, steps in PLAN:
            if where == place:
                out = work(*steps)
                x, y, _ = lax.optimization_barrier((x, y, out))
        return x, y

    for s in range(1, HALF):
        na, nb = ring_step(*ties(f"n{s}", na, nb))
        oa, ob = ring_step(*ties(f"o{s}", oa, ob))
        near[s], near[NZ - s] = na, nb
        over[s], over[NZ - s] = oa, ob
    near_half, over_half = n // 3, n - n // 3
    na, nb = ties("n4", na, nb)
    near[HALF] = ring_step(na[near_half:], nb[:near_half])
    oa, ob = ties("o4", oa, ob)
    over[HALF] = ring_step(oa[over_half:], ob[:over_half])
    work(*LAST)
    if 0 not in done_near:
        work(0)
    own, at = done_near[0]
    own = own[at : at + 2 * n]
    sums_near = ring_reduce(done_near, n, near_half, *([own] if OWN_LAST else []))
    sums_over = ring_reduce(done_over, n, over_half)
    ready = call(
        close_kernel,
        jax.ShapeDtypeStruct((NX,) + cut.shape, bf16),
        (xl[None], own) + sums_near + sums_over,
        smem=1,
        name="close",
    )
    back = lax.all_to_all(
        ready.reshape((NX * EXPERTS,) + cut.shape[1:]),
        ("xl",) + EXP,
        split_axis=0,
        concat_axis=0,
        tiled=True,
    ).reshape(ready.shape)
    return call(
        mix_kernel,
        jax.ShapeDtypeStruct((tok_dev, width), bf16),
        (hstate, combine, back),
        name="mix",
    )


def solution(mesh):
    fine = Mesh(mesh.devices.reshape(NX, NZ, NC, NH, NY), CTX + EXP)
    placed = (
        P(CTX, EXP),
        P(CTX, EXP),
        P(CTX, EXP),
        P(EXP, CTX),
        P(CTX + EXP, None),
        P(),
        P(EXP, None, CTX),
        P(EXP, None, CTX),
        P(EXP, CTX, None),
        P(CTX + EXP, None),
        P(CTX + EXP, None),
    )
    return jax.shard_map(
        shards, mesh=fine, in_specs=placed, out_specs=P(CTX + EXP, None), check_vma=False
    )
```

```python
import functools
import math

import jax
import jax.numpy as jnp
from jax import lax
from jax.experimental import pallas as pl
from jax.experimental.pallas import tpu as pltpu
from jax.sharding import Mesh
from jax.sharding import PartitionSpec as P

HD = 128
EXPERTS = 8
NX, NZ, NC, NH, NY = 2, 8, 2, 2, 4
CTX = ("xl", "z", "c")
EXP = ("xh", "y")
SEQ_BLOCKS = NX * NZ * NC
SWAP = [(0, 1), (1, 0)]
bf16 = jnp.bfloat16
f32 = jnp.float32


HALF = NZ // 2
PLAN = [('o2', (0,)), ('o3', (1,)), ('n4', (2,)), ('over', (3,))]
LAST = (4,)
OWN_LAST = False


def even(x):
    return lax.ppermute(x, "z", [(i, i ^ 1) for i in range(NZ)])


def odd(x):
    return lax.ppermute(x, "z", [(i, (i + 1 if i % 2 else i - 1) % NZ) for i in range(NZ)])


def add_kernel(first, rows, p_ref, q_ref, o_ref):
    p = p_ref[first : first + o_ref.shape[0], :]
    at, size = rows
    if size < o_ref.shape[0]:
        o_ref[...] = p
    o_ref[at : at + size, :] = (
        p[at : at + size].astype(f32) + q_ref[...].astype(f32)
    ).astype(bf16)


def add(term, rows, q, at=0):
    block, first = term
    return call(
        functools.partial(add_kernel, first, (at, q.shape[0])),
        jax.ShapeDtypeStruct((rows, q.shape[1]), bf16),
        (block, q),
        name="add",
    )


def ring_reduce(parts, rows, half, *after):
    far, at = parts[HALF]
    ra, rb = even(far[at : at + half]), odd(far[at + half : at + rows])
    for s in range(HALF - 1, 0, -1):
        last = s == HALF - 1
        sa = add(parts[s], rows, rb, half if last else 0)
        sb = add(parts[NZ - s], rows, ra)
        if after and s == 1:
            sa, sb, *_ = lax.optimization_barrier((sa, sb) + after)
        ra, rb = even(sa), odd(sb)
    return ra, rb


def experts_kernel(x_ref, g0, u0, d0, g1, u1, d1, o_ref, wg, wu, wd, sem):
    copies = []
    for p, (g, u, d) in enumerate(((g0, u0, d0), (g1, u1, d1))):
        for k, (src, dst) in enumerate(((g, wg), (u, wu), (d, wd))):
            copies.append(pltpu.make_async_copy(src, dst.at[p], sem.at[3 * p + k]))
    for copy in copies:
        copy.start()
    x = x_ref[...]
    out = None
    for p in range(2):
        copies[3 * p].wait()
        gate = jnp.dot(x, wg[p], preferred_element_type=f32)
        copies[3 * p + 1].wait()
        upper = jnp.dot(x, wu[p], preferred_element_type=f32)
        act = (gate / (1.0 + jnp.exp(-gate)) * upper).astype(bf16)
        copies[3 * p + 2].wait()
        down = jnp.dot(act, wd[p], preferred_element_type=f32)
        out = down if out is None else out + down
    o_ref[...] = out.astype(bf16)


def run_experts(x, weights):
    rows, width = x.shape
    ff = weights[0].shape[1]
    hbm = pl.BlockSpec(memory_space=pl.ANY)
    vmem = pl.BlockSpec(memory_space=pltpu.VMEM)
    return pl.pallas_call(
        experts_kernel,
        out_shape=jax.ShapeDtypeStruct((rows, width), bf16),
        in_specs=[vmem] + [hbm] * 6,
        out_specs=vmem,
        scratch_shapes=[
            pltpu.VMEM((2, width, ff), bf16),
            pltpu.VMEM((2, width, ff), bf16),
            pltpu.VMEM((2, ff, width), bf16),
            pltpu.SemaphoreType.DMA((6,)),
        ],
        compiler_params=pltpu.CompilerParams(vmem_limit_bytes=40 * 1024 * 1024),
        cost_estimate=pl.CostEstimate(
            flops=2 * 6 * rows * width * ff,
            bytes_accessed=12 * width * ff + 4 * rows * width,
            transcendentals=2 * rows * ff,
        ),
        name="experts",
    )(x, *weights)


def call(kernel, out_shape, args, smem=0, mib=24, name=None, **kw):
    vmem = pl.BlockSpec(memory_space=pltpu.VMEM)
    return pl.pallas_call(
        kernel,
        out_shape=out_shape,
        in_specs=[pl.BlockSpec(memory_space=pltpu.SMEM)] * smem + [vmem] * (len(args) - smem),
        out_specs=jax.tree.map(lambda _: vmem, out_shape),
        compiler_params=pltpu.CompilerParams(vmem_limit_bytes=mib * 1024 * 1024),
        name=name,
        **kw,
    )(*args)


def pack_kernel(k0, v0, w0, k1, v1, w1, o_ref, sem):
    rows, deep = k0.shape[0], w0.shape[0]
    copies = []
    for i, ref in enumerate((k0, v0, k1, v1, w0, w1)):
        r, c = divmod(i, 2)
        first, size = (r * rows, rows) if r < 2 else (2 * rows, deep)
        to = o_ref.at[first : first + size, c * HD : (c + 1) * HD]
        copies.append(pltpu.make_async_copy(ref, to, sem.at[i]))
    for copy in copies:
        copy.start()
    for copy in copies:
        copy.wait()


def attend_kernel(first, starts, q_ref, *refs):
    cores = len(refs) - 7
    blocks, (o_hbm, kv_all, w_all, o_ref, sem_k, sem_w, sem_o) = refs[:cores], refs[cores:]
    rows, group = q_ref.shape[0], q_ref.shape[1] // HD
    deep, wide = w_all.shape[2], w_all.shape[3]
    pair = 2 * rows
    waits_k, waits_w = [], []
    for i, ref in enumerate(blocks):
        core, r = divmod(i, NZ + 1)
        at = min(r, HALF) if r <= HALF else r - 1
        low = r == HALF + 1
        if not low:
            to = slice((core * NZ + at) * pair, (core * NZ + at + 1) * pair)
            waits_k.append(
                pltpu.make_async_copy(ref.at[:pair, :], kv_all.at[to, :], sem_k.at[len(waits_k)])
            )
        skip = 0 if low else pair
        size = ref.shape[0] - skip
        begin = deep - size if low else 0
        waits_w.append(
            pltpu.make_async_copy(
                ref.at[skip:, :], w_all.at[core, at, begin : begin + size, :], sem_w.at[i]
            )
        )
    for copy in waits_k + waits_w:
        copy.start()
    q = jnp.concatenate([q_ref[:, h * HD : (h + 1) * HD] for h in range(group)], axis=0)
    q_position = first[0] + lax.broadcasted_iota(jnp.int32, (rows, 1), 0)
    q_position = jnp.concatenate([q_position] * group, axis=0)
    scale = 1.0 / math.sqrt(HD)
    for copy in waits_k:
        copy.wait()
    part = NZ * pair
    column = lax.broadcasted_iota(jnp.int32, (1, part), 1)
    scores = []
    for core in range(NC):
        s = lax.dot_general(
            q,
            kv_all[core * part : (core + 1) * part, :HD],
            (((1,), (1,)), ((), ())),
            preferred_element_type=f32,
        )
        shift = jnp.zeros((1, part), jnp.int32)
        for j in range(2 * NZ):
            shift = jnp.where(column >= j * rows, starts[core * 2 * NZ + j] - j * rows, shift)
        scores.append(jnp.where(column + shift <= q_position, s * scale, -1e30))
    top = jnp.maximum(*[jnp.max(s, axis=-1, keepdims=True) for s in scores])
    total, acc = 0.0, 0.0
    for core, s in enumerate(scores):
        w = jnp.exp(s - top)
        total = total + jnp.sum(w, axis=-1, keepdims=True)
        acc = acc + jnp.dot(
            w.astype(bf16),
            kv_all[core * part : (core + 1) * part, HD:],
            preferred_element_type=f32,
        )
    heads = (acc / total).astype(bf16)
    heads = jnp.concatenate([heads[h * rows : (h + 1) * rows] for h in range(group)], axis=1)
    for copy in waits_w:
        copy.wait()
    tok = rows // EXPERTS
    out = []
    for r in range(NZ):
        p = [
            jnp.dot(heads, w_all[core, r], preferred_element_type=f32) for core in range(NC)
        ]
        for e in range(EXPERTS):
            both = jnp.concatenate([x[e * tok : (e + 1) * tok] for x in p], axis=0)
            o_ref[e, :, r * wide : (r + 1) * wide] = both.astype(bf16)
        to = slice(r * wide, (r + 1) * wide)
        copy = pltpu.make_async_copy(o_ref.at[:, :, to], o_hbm.at[:, :, to], sem_o.at[r])
        copy.start()
        out.append(copy)
    for copy in out:
        copy.wait()


def tail_kernel(src_ref, parts_ref, residual_ref, gain_ref, placing_ref, h_ref, o_ref, sum_ref):
    rows, width = h_ref.shape
    half = width // 2
    total = parts_ref[0].astype(f32)
    for e in range(1, EXPERTS):
        total = total + parts_ref[e].astype(f32)
    sum_ref[:, :half] = total[:rows]
    sum_ref[:, half:] = total[rows:]
    for j in range(width // HD):
        lanes = pl.ds(pl.multiple_of(src_ref[j] * HD, HD), HD)
        to = slice(j * HD, (j + 1) * HD)
        h_ref[:, to] = residual_ref[:, to].astype(f32) + sum_ref[:, lanes]
    h = h_ref[...]
    meansq = jnp.mean(h * h, axis=-1, keepdims=True)
    normed = (h * lax.rsqrt(meansq + 1e-05) * gain_ref[...]).astype(bf16)
    cut_rows(jnp.dot(placing_ref[...], normed, preferred_element_type=f32), o_ref)


def cut_rows(x, o_ref):
    cap = x.shape[0] // EXPERTS
    cuts, piece = o_ref.shape[1] // cap, o_ref.shape[2]
    for e in range(EXPERTS):
        rows = x[e * cap : (e + 1) * cap]
        o_ref[e] = jnp.concatenate(
            [rows[:, i * piece : (i + 1) * piece] for i in range(cuts)], axis=0
        ).astype(bf16)


def join_rows(x_ref, cap):
    cuts = x_ref.shape[1] // cap
    blocks = [x_ref[e].astype(f32) for e in range(EXPERTS)]
    return jnp.concatenate(
        [
            jnp.concatenate([x[i * cap : (i + 1) * cap] for i in range(cuts)], axis=1)
            for x in blocks
        ],
        axis=0,
    )


def join_kernel(x_ref, o_ref):
    o_ref[...] = join_rows(x_ref, o_ref.shape[0] // EXPERTS).astype(bf16)


def close_kernel(xl, own_ref, na, nb, oa, ob, o_ref):
    n = na.shape[0]
    for i, (a, b) in enumerate(((na, nb), (oa, ob))):
        total = own_ref[i * n : (i + 1) * n, :].astype(f32) + a[...].astype(f32)
        total = total + b[...].astype(f32)
        cut_rows(total, o_ref.at[xl[0] if i == 0 else 1 - xl[0]])


def mix_kernel(h_ref, combine_ref, back_ref, o_ref):
    cap = combine_ref.shape[1] // EXPERTS
    rows = join_rows(back_ref.at[0], cap) + join_rows(back_ref.at[1], cap)
    mixed = jnp.dot(
        combine_ref[...], rows, precision=lax.Precision.HIGHEST, preferred_element_type=f32
    )
    o_ref[...] = (h_ref[...] + mixed).astype(bf16)


def shards(
    queries,
    keys,
    values,
    out_weight,
    residual,
    norm_gain,
    gate_weight,
    up_weight,
    down_weight,
    route_ids,
    route_weight,
):
    xl, z, c = lax.axis_index("xl"), lax.axis_index("z"), lax.axis_index("c")
    tok_blk = queries.shape[0]
    group = queries.shape[1] // HD
    width = residual.shape[1]
    ctx = (xl * NZ + z) * NC + c
    block_first = ctx * tok_blk

    def other_x(x):
        return lax.ppermute(x, "xl", SWAP)

    def other_core(x):
        return lax.ppermute(x, "c", SWAP)

    def ring_step(a, b, *after):
        if after:
            a, b, *_ = lax.optimization_barrier((a, b) + after)
        return even(b), odd(a)

    theirs = other_x(keys), other_x(values), other_x(out_weight)
    own = pl.pallas_call(
        pack_kernel,
        out_shape=jax.ShapeDtypeStruct((2 * tok_blk + out_weight.shape[0], 2 * HD), bf16),
        in_specs=[pl.BlockSpec(memory_space=pl.ANY)] * 6,
        out_specs=pl.BlockSpec(memory_space=pltpu.VMEM),
        compiler_params=pltpu.CompilerParams(vmem_limit_bytes=4 * 1024 * 1024),
        scratch_shapes=[pltpu.SemaphoreType.DMA((6,))],
        name="pack",
    )(keys, values, out_weight, *theirs)
    half = own.shape[0] // 2
    came = [own] + [None] * (NZ - 1)
    a = b = own
    for s in range(1, HALF):
        a, b = ring_step(a, b)
        came[s], came[NZ - s] = a, b
    came[HALF : HALF + 1] = ring_step(a[half:], b[:half])
    came = came + [other_core(x) for x in came]

    core_of = jnp.stack([c, 1 - c])[:, None, None]
    turn = 1 - 2 * (z % 2)
    z_of = ((z + turn * jnp.arange(NZ, dtype=jnp.int32)) % NZ)[None, :, None]
    x_of = jnp.stack([xl, 1 - xl])[None, None, :]
    starts = (((x_of * NZ + z_of) * NC + core_of) * tok_blk).reshape(-1)
    keys_all = SEQ_BLOCKS * tok_blk
    tok_dev = residual.shape[0]
    deep = out_weight.shape[0]
    hbm = pl.BlockSpec(memory_space=pl.ANY)
    smem = pl.BlockSpec(memory_space=pltpu.SMEM)
    part_shape = (EXPERTS, 2 * tok_dev, width // 2)
    part = pl.pallas_call(
        attend_kernel,
        out_shape=jax.ShapeDtypeStruct(part_shape, bf16),
        in_specs=[smem, smem, pl.BlockSpec(memory_space=pltpu.VMEM)] + [hbm] * len(came),
        out_specs=hbm,
        scratch_shapes=[
            pltpu.VMEM((keys_all, 2 * HD), bf16),
            pltpu.VMEM((NC, NZ, deep, 2 * HD), bf16),
            pltpu.VMEM(part_shape, bf16),
            pltpu.SemaphoreType.DMA((2 * NZ,)),
            pltpu.SemaphoreType.DMA((len(came),)),
            pltpu.SemaphoreType.DMA((NZ,)),
        ],
        compiler_params=pltpu.CompilerParams(vmem_limit_bytes=60 * 1024 * 1024),
        cost_estimate=pl.CostEstimate(
            flops=4 * tok_blk * group * HD * keys_all + 2 * tok_blk * deep * width,
            bytes_accessed=4 * HD * keys_all + 2 * deep * width,
            transcendentals=tok_blk * group * keys_all,
        ),
        name="attend",
    )(block_first[None], starts, queries, *came)
    panels = lax.optimization_barrier((gate_weight[0], up_weight[0], down_weight[0], part))
    part = panels[3]
    panels_o = tuple(other_core(x) for x in panels[:3])
    parts = lax.all_to_all(part, EXP, split_axis=0, concat_axis=0, tiled=True)
    parts, *panels_o = lax.optimization_barrier((parts,) + panels_o)
    xs = jnp.arange(NX, dtype=jnp.int32)[:, None, None]
    zs = jnp.arange(NZ, dtype=jnp.int32)[None, :, None]
    cs = jnp.arange(NC, dtype=jnp.int32)[None, None, :]
    source = (((cs ^ c) * NZ + (turn * (zs - z)) % NZ) * NX + (xs ^ xl)).reshape(-1)

    picks = route_ids.shape[1]
    cap = 2 * tok_dev * picks // EXPERTS
    flat_ids = route_ids.reshape(-1)
    onehot = (flat_ids[:, None] == jnp.arange(EXPERTS, dtype=jnp.int32)[None, :]).astype(jnp.int32)
    earlier = jnp.cumsum(onehot, axis=0) - onehot
    slot = jnp.sum(earlier * onehot, axis=1)
    place = flat_ids * cap + slot
    hits = (
        jnp.arange(EXPERTS * cap, dtype=jnp.int32)[None, :] == place[:, None]
    ).reshape(tok_dev, picks, EXPERTS * cap)
    placing = jnp.any(hits, axis=1).astype(bf16).T
    combine = jnp.sum(jnp.where(hits, route_weight[:, :, None], 0.0), axis=1)
    n = EXPERTS * cap
    cuts = 4
    cut = jax.ShapeDtypeStruct((EXPERTS, cuts * cap, width // cuts), bf16)
    hstate, outgoing = call(
        tail_kernel,
        (jax.ShapeDtypeStruct((tok_dev, width), f32), cut),
        (source, parts, residual, norm_gain[None, :], placing),
        smem=1,
        mib=60,
        name="tail",
        scratch_shapes=[pltpu.VMEM((tok_dev, width), f32)],
    )
    rows = call(
        join_kernel,
        jax.ShapeDtypeStruct((n, width), bf16),
        (lax.all_to_all(outgoing, EXP, split_axis=0, concat_axis=0, tiled=True),),
        name="join",
    )

    panels = (gate_weight[0], up_weight[0], down_weight[0], *panels_o)
    near, over = [None] * NZ, [None] * NZ
    near[0], over[0] = rows, other_x(rows)
    done_near, done_over = {}, {}

    def work(*steps):
        blocks = []
        for s in steps:
            if s == 0:
                pieces = [(near[0],), (over[0],)]
            elif s == HALF:
                pieces = [near[s], over[s]]
            else:
                pieces = [(near[s],), (near[NZ - s],), (over[s],), (over[NZ - s],)]
            blocks += [x for piece in pieces for x in piece]
        out = run_experts(jnp.concatenate(blocks, axis=0), panels)
        at = 0
        for s in steps:
            if s in (0, HALF):
                done_near[s], done_over[s] = (out, at), (out, at + n)
                at += 2 * n
            else:
                done_near[s], done_near[NZ - s] = (out, at), (out, at + n)
                done_over[s], done_over[NZ - s] = (out, at + 2 * n), (out, at + 3 * n)
                at += 4 * n
        return out

    na = nb = near[0]
    oa = ob = over[0]
    outs = []

    def ties(place, x, y):
        for where, steps in PLAN:
            if where == place:
                out = work(*steps)
                x, y, _ = lax.optimization_barrier((x, y, out))
        return x, y

    for s in range(1, HALF):
        na, nb = ring_step(*ties(f"n{s}", na, nb))
        oa, ob = ring_step(*ties(f"o{s}", oa, ob))
        near[s], near[NZ - s] = na, nb
        over[s], over[NZ - s] = oa, ob
    near_half, over_half = n // 3, n - n // 3
    na, nb = ties("n4", na, nb)
    near[HALF] = ring_step(na[near_half:], nb[:near_half])
    oa, ob = ties("o4", oa, ob)
    over[HALF] = ring_step(oa[over_half:], ob[:over_half])
    near[HALF] = ties("near", *near[HALF])
    over[HALF] = ties("over", *over[HALF])
    work(*LAST)
    if 0 not in done_near:
        work(0)
    own, at = done_near[0]
    own = own[at : at + 2 * n]
    sums_near = ring_reduce(done_near, n, near_half, *([own] if OWN_LAST else []))
    sums_over = ring_reduce(done_over, n, over_half)
    ready = call(
        close_kernel,
        jax.ShapeDtypeStruct((NX,) + cut.shape, bf16),
        (xl[None], own) + sums_near + sums_over,
        smem=1,
        name="close",
    )
    back = lax.all_to_all(
        ready.reshape((NX * EXPERTS,) + cut.shape[1:]),
        ("xl",) + EXP,
        split_axis=0,
        concat_axis=0,
        tiled=True,
    ).reshape(ready.shape)
    return call(
        mix_kernel,
        jax.ShapeDtypeStruct((tok_dev, width), bf16),
        (hstate, combine, back),
        name="mix",
    )


def solution(mesh):
    fine = Mesh(mesh.devices.reshape(NX, NZ, NC, NH, NY), CTX + EXP)
    placed = (
        P(CTX, EXP),
        P(CTX, EXP),
        P(CTX, EXP),
        P(EXP, CTX),
        P(CTX + EXP, None),
        P(),
        P(EXP, None, CTX),
        P(EXP, None, CTX),
        P(EXP, CTX, None),
        P(CTX + EXP, None),
        P(CTX + EXP, None),
    )
    return jax.shard_map(
        shards, mesh=fine, in_specs=placed, out_specs=P(CTX + EXP, None), check_vma=False
    )
```

```python
import functools
import math

import jax
import jax.numpy as jnp
from jax import lax
from jax.experimental import pallas as pl
from jax.experimental.pallas import tpu as pltpu
from jax.sharding import Mesh
from jax.sharding import PartitionSpec as P

HD = 128
EXPERTS = 8
NX, NZ, NC, NH, NY = 2, 8, 2, 2, 4
CTX = ("xl", "z", "c")
EXP = ("xh", "y")
SEQ_BLOCKS = NX * NZ * NC
SWAP = [(0, 1), (1, 0)]
bf16 = jnp.bfloat16
f32 = jnp.float32


HALF = NZ // 2
PLAN = [('o2', (0,)), ('o3', (1,)), ('n4', (2,)), ('over', (3,))]
LAST = (4,)
OWN_LAST = False


def even(x):
    return lax.ppermute(x, "z", [(i, i ^ 1) for i in range(NZ)])


def odd(x):
    return lax.ppermute(x, "z", [(i, (i + 1 if i % 2 else i - 1) % NZ) for i in range(NZ)])


def add_kernel(first, rows, p_ref, q_ref, o_ref):
    p = p_ref[first : first + o_ref.shape[0], :]
    at, size = rows
    if size < o_ref.shape[0]:
        o_ref[...] = p
    o_ref[at : at + size, :] = (
        p[at : at + size].astype(f32) + q_ref[...].astype(f32)
    ).astype(bf16)


def add(term, rows, q, at=0):
    block, first = term
    return call(
        functools.partial(add_kernel, first, (at, q.shape[0])),
        jax.ShapeDtypeStruct((rows, q.shape[1]), bf16),
        (block, q),
        name="add",
    )


def ring_reduce(parts, rows, half, *after):
    far, at = parts[HALF]
    ra, rb = even(far[at : at + half]), odd(far[at + half : at + rows])
    for s in range(HALF - 1, 0, -1):
        last = s == HALF - 1
        sa = add(parts[s], rows, rb, half if last else 0)
        sb = add(parts[NZ - s], rows, ra)
        if after and s == 1:
            sa, sb, *_ = lax.optimization_barrier((sa, sb) + after)
        ra, rb = even(sa), odd(sb)
    return ra, rb


def experts_kernel(x_ref, g0, u0, d0, g1, u1, d1, o_ref, wg, wu, wd, sem):
    copies = []
    for p, (g, u, d) in enumerate(((g0, u0, d0), (g1, u1, d1))):
        for k, (src, dst) in enumerate(((g, wg), (u, wu), (d, wd))):
            copies.append(pltpu.make_async_copy(src, dst.at[p], sem.at[3 * p + k]))
    for copy in copies:
        copy.start()
    x = x_ref[...]
    out = None
    for p in range(2):
        copies[3 * p].wait()
        gate = jnp.dot(x, wg[p], preferred_element_type=f32)
        copies[3 * p + 1].wait()
        upper = jnp.dot(x, wu[p], preferred_element_type=f32)
        act = (gate / (1.0 + jnp.exp(-gate)) * upper).astype(bf16)
        copies[3 * p + 2].wait()
        down = jnp.dot(act, wd[p], preferred_element_type=f32)
        out = down if out is None else out + down
    o_ref[...] = out.astype(bf16)


def run_experts(x, weights):
    rows, width = x.shape
    ff = weights[0].shape[1]
    hbm = pl.BlockSpec(memory_space=pl.ANY)
    vmem = pl.BlockSpec(memory_space=pltpu.VMEM)
    return pl.pallas_call(
        experts_kernel,
        out_shape=jax.ShapeDtypeStruct((rows, width), bf16),
        in_specs=[vmem] + [hbm] * 6,
        out_specs=vmem,
        scratch_shapes=[
            pltpu.VMEM((2, width, ff), bf16),
            pltpu.VMEM((2, width, ff), bf16),
            pltpu.VMEM((2, ff, width), bf16),
            pltpu.SemaphoreType.DMA((6,)),
        ],
        compiler_params=pltpu.CompilerParams(vmem_limit_bytes=31 * 1024 * 1024),
        cost_estimate=pl.CostEstimate(
            flops=2 * 6 * rows * width * ff,
            bytes_accessed=12 * width * ff + 4 * rows * width,
            transcendentals=2 * rows * ff,
        ),
        name="experts",
    )(x, *weights)


def call(kernel, out_shape, args, smem=0, mib=24, name=None, **kw):
    vmem = pl.BlockSpec(memory_space=pltpu.VMEM)
    return pl.pallas_call(
        kernel,
        out_shape=out_shape,
        in_specs=[pl.BlockSpec(memory_space=pltpu.SMEM)] * smem + [vmem] * (len(args) - smem),
        out_specs=jax.tree.map(lambda _: vmem, out_shape),
        compiler_params=pltpu.CompilerParams(vmem_limit_bytes=mib * 1024 * 1024),
        name=name,
        **kw,
    )(*args)


def pack_kernel(k0, v0, w0, k1, v1, w1, o_ref, sem):
    rows, deep = k0.shape[0], w0.shape[0]
    copies = []
    for i, ref in enumerate((k0, v0, k1, v1, w0, w1)):
        r, c = divmod(i, 2)
        first, size = (r * rows, rows) if r < 2 else (2 * rows, deep)
        to = o_ref.at[first : first + size, c * HD : (c + 1) * HD]
        copies.append(pltpu.make_async_copy(ref, to, sem.at[i]))
    for copy in copies:
        copy.start()
    for copy in copies:
        copy.wait()


def attend_kernel(first, starts, q_ref, *refs):
    cores = len(refs) - 7
    blocks, (o_hbm, kv_all, w_all, o_ref, sem_k, sem_w, sem_o) = refs[:cores], refs[cores:]
    rows, group = q_ref.shape[0], q_ref.shape[1] // HD
    deep, wide = w_all.shape[2], w_all.shape[3]
    pair = 2 * rows
    waits_k, waits_w = [], []
    for i, ref in enumerate(blocks):
        core, r = divmod(i, NZ + 1)
        at = min(r, HALF) if r <= HALF else r - 1
        low = r == HALF + 1
        if not low:
            to = slice((core * NZ + at) * pair, (core * NZ + at + 1) * pair)
            waits_k.append(
                pltpu.make_async_copy(ref.at[:pair, :], kv_all.at[to, :], sem_k.at[len(waits_k)])
            )
        skip = 0 if low else pair
        size = ref.shape[0] - skip
        begin = deep - size if low else 0
        waits_w.append(
            pltpu.make_async_copy(
                ref.at[skip:, :], w_all.at[core, at, begin : begin + size, :], sem_w.at[i]
            )
        )
    for copy in waits_k + waits_w:
        copy.start()
    q = jnp.concatenate([q_ref[:, h * HD : (h + 1) * HD] for h in range(group)], axis=0)
    q_position = first[0] + lax.broadcasted_iota(jnp.int32, (rows, 1), 0)
    q_position = jnp.concatenate([q_position] * group, axis=0)
    scale = 1.0 / math.sqrt(HD)
    for copy in waits_k:
        copy.wait()
    part = NZ * pair
    column = lax.broadcasted_iota(jnp.int32, (1, part), 1)
    scores = []
    for core in range(NC):
        s = lax.dot_general(
            q,
            kv_all[core * part : (core + 1) * part, :HD],
            (((1,), (1,)), ((), ())),
            preferred_element_type=f32,
        )
        shift = jnp.zeros((1, part), jnp.int32)
        for j in range(2 * NZ):
            shift = jnp.where(column >= j * rows, starts[core * 2 * NZ + j] - j * rows, shift)
        scores.append(jnp.where(column + shift <= q_position, s * scale, -1e30))
    top = jnp.maximum(*[jnp.max(s, axis=-1, keepdims=True) for s in scores])
    total, acc = 0.0, 0.0
    for core, s in enumerate(scores):
        w = jnp.exp(s - top)
        total = total + jnp.sum(w, axis=-1, keepdims=True)
        acc = acc + jnp.dot(
            w.astype(bf16),
            kv_all[core * part : (core + 1) * part, HD:],
            preferred_element_type=f32,
        )
    heads = (acc / total).astype(bf16)
    heads = jnp.concatenate([heads[h * rows : (h + 1) * rows] for h in range(group)], axis=1)
    for copy in waits_w:
        copy.wait()
    tok = rows // EXPERTS
    out = []
    for r in range(NZ):
        p = [
            jnp.dot(heads, w_all[core, r], preferred_element_type=f32) for core in range(NC)
        ]
        for e in range(EXPERTS):
            both = jnp.concatenate([x[e * tok : (e + 1) * tok] for x in p], axis=0)
            o_ref[e, :, r * wide : (r + 1) * wide] = both.astype(bf16)
        to = slice(r * wide, (r + 1) * wide)
        copy = pltpu.make_async_copy(o_ref.at[:, :, to], o_hbm.at[:, :, to], sem_o.at[r])
        copy.start()
        out.append(copy)
    for copy in out:
        copy.wait()


def tail_kernel(src_ref, parts_ref, residual_ref, gain_ref, placing_ref, h_ref, o_ref, sum_ref):
    rows, width = h_ref.shape
    half = width // 2
    total = parts_ref[0].astype(f32)
    for e in range(1, EXPERTS):
        total = total + parts_ref[e].astype(f32)
    sum_ref[:, :half] = total[:rows]
    sum_ref[:, half:] = total[rows:]
    for j in range(width // HD):
        lanes = pl.ds(pl.multiple_of(src_ref[j] * HD, HD), HD)
        to = slice(j * HD, (j + 1) * HD)
        h_ref[:, to] = residual_ref[:, to].astype(f32) + sum_ref[:, lanes]
    h = h_ref[...]
    meansq = jnp.mean(h * h, axis=-1, keepdims=True)
    normed = (h * lax.rsqrt(meansq + 1e-05) * gain_ref[...]).astype(bf16)
    cut_rows(jnp.dot(placing_ref[...], normed, preferred_element_type=f32), o_ref)


def cut_rows(x, o_ref):
    cap = x.shape[0] // EXPERTS
    cuts, piece = o_ref.shape[1] // cap, o_ref.shape[2]
    for e in range(EXPERTS):
        rows = x[e * cap : (e + 1) * cap]
        o_ref[e] = jnp.concatenate(
            [rows[:, i * piece : (i + 1) * piece] for i in range(cuts)], axis=0
        ).astype(bf16)


def join_rows(x_ref, cap):
    cuts = x_ref.shape[1] // cap
    blocks = [x_ref[e].astype(f32) for e in range(EXPERTS)]
    return jnp.concatenate(
        [
            jnp.concatenate([x[i * cap : (i + 1) * cap] for i in range(cuts)], axis=1)
            for x in blocks
        ],
        axis=0,
    )


def join_kernel(x_ref, o_ref):
    o_ref[...] = join_rows(x_ref, o_ref.shape[0] // EXPERTS).astype(bf16)


def close_kernel(xl, own_ref, na, nb, oa, ob, o_ref):
    n = na.shape[0]
    for i, (a, b) in enumerate(((na, nb), (oa, ob))):
        total = own_ref[i * n : (i + 1) * n, :].astype(f32) + a[...].astype(f32)
        total = total + b[...].astype(f32)
        cut_rows(total, o_ref.at[xl[0] if i == 0 else 1 - xl[0]])


def mix_kernel(h_ref, combine_ref, back_ref, o_ref):
    cap = combine_ref.shape[1] // EXPERTS
    rows = join_rows(back_ref.at[0], cap) + join_rows(back_ref.at[1], cap)
    mixed = jnp.dot(
        combine_ref[...], rows, precision=lax.Precision.HIGHEST, preferred_element_type=f32
    )
    o_ref[...] = (h_ref[...] + mixed).astype(bf16)


def shards(
    queries,
    keys,
    values,
    out_weight,
    residual,
    norm_gain,
    gate_weight,
    up_weight,
    down_weight,
    route_ids,
    route_weight,
):
    xl, z, c = lax.axis_index("xl"), lax.axis_index("z"), lax.axis_index("c")
    tok_blk = queries.shape[0]
    group = queries.shape[1] // HD
    width = residual.shape[1]
    ctx = (xl * NZ + z) * NC + c
    block_first = ctx * tok_blk

    def other_x(x):
        return lax.ppermute(x, "xl", SWAP)

    def other_core(x):
        return lax.ppermute(x, "c", SWAP)

    def ring_step(a, b, *after):
        if after:
            a, b, *_ = lax.optimization_barrier((a, b) + after)
        return even(b), odd(a)

    theirs = other_x(keys), other_x(values), other_x(out_weight)
    own = pl.pallas_call(
        pack_kernel,
        out_shape=jax.ShapeDtypeStruct((2 * tok_blk + out_weight.shape[0], 2 * HD), bf16),
        in_specs=[pl.BlockSpec(memory_space=pl.ANY)] * 6,
        out_specs=pl.BlockSpec(memory_space=pltpu.VMEM),
        compiler_params=pltpu.CompilerParams(vmem_limit_bytes=4 * 1024 * 1024),
        scratch_shapes=[pltpu.SemaphoreType.DMA((6,))],
        name="pack",
    )(keys, values, out_weight, *theirs)
    half = own.shape[0] // 2
    came = [own] + [None] * (NZ - 1)
    a = b = own
    for s in range(1, HALF):
        a, b = ring_step(a, b)
        came[s], came[NZ - s] = a, b
    came[HALF : HALF + 1] = ring_step(a[half:], b[:half])
    came = came + [other_core(x) for x in came]

    core_of = jnp.stack([c, 1 - c])[:, None, None]
    turn = 1 - 2 * (z % 2)
    z_of = ((z + turn * jnp.arange(NZ, dtype=jnp.int32)) % NZ)[None, :, None]
    x_of = jnp.stack([xl, 1 - xl])[None, None, :]
    starts = (((x_of * NZ + z_of) * NC + core_of) * tok_blk).reshape(-1)
    keys_all = SEQ_BLOCKS * tok_blk
    tok_dev = residual.shape[0]
    deep = out_weight.shape[0]
    hbm = pl.BlockSpec(memory_space=pl.ANY)
    smem = pl.BlockSpec(memory_space=pltpu.SMEM)
    part_shape = (EXPERTS, 2 * tok_dev, width // 2)
    part = pl.pallas_call(
        attend_kernel,
        out_shape=jax.ShapeDtypeStruct(part_shape, bf16),
        in_specs=[smem, smem, pl.BlockSpec(memory_space=pltpu.VMEM)] + [hbm] * len(came),
        out_specs=hbm,
        scratch_shapes=[
            pltpu.VMEM((keys_all, 2 * HD), bf16),
            pltpu.VMEM((NC, NZ, deep, 2 * HD), bf16),
            pltpu.VMEM(part_shape, bf16),
            pltpu.SemaphoreType.DMA((2 * NZ,)),
            pltpu.SemaphoreType.DMA((len(came),)),
            pltpu.SemaphoreType.DMA((NZ,)),
        ],
        compiler_params=pltpu.CompilerParams(vmem_limit_bytes=60 * 1024 * 1024),
        cost_estimate=pl.CostEstimate(
            flops=4 * tok_blk * group * HD * keys_all + 2 * tok_blk * deep * width,
            bytes_accessed=4 * HD * keys_all + 2 * deep * width,
            transcendentals=tok_blk * group * keys_all,
        ),
        name="attend",
    )(block_first[None], starts, queries, *came)
    panels = lax.optimization_barrier((gate_weight[0], up_weight[0], down_weight[0], part))
    part = panels[3]
    panels_o = tuple(other_core(x) for x in panels[:3])
    parts = lax.all_to_all(part, EXP, split_axis=0, concat_axis=0, tiled=True)
    parts, *panels_o = lax.optimization_barrier((parts,) + panels_o)
    xs = jnp.arange(NX, dtype=jnp.int32)[:, None, None]
    zs = jnp.arange(NZ, dtype=jnp.int32)[None, :, None]
    cs = jnp.arange(NC, dtype=jnp.int32)[None, None, :]
    source = (((cs ^ c) * NZ + (turn * (zs - z)) % NZ) * NX + (xs ^ xl)).reshape(-1)

    picks = route_ids.shape[1]
    cap = 2 * tok_dev * picks // EXPERTS
    flat_ids = route_ids.reshape(-1)
    onehot = (flat_ids[:, None] == jnp.arange(EXPERTS, dtype=jnp.int32)[None, :]).astype(jnp.int32)
    earlier = jnp.cumsum(onehot, axis=0) - onehot
    slot = jnp.sum(earlier * onehot, axis=1)
    place = flat_ids * cap + slot
    hits = (
        jnp.arange(EXPERTS * cap, dtype=jnp.int32)[None, :] == place[:, None]
    ).reshape(tok_dev, picks, EXPERTS * cap)
    placing = jnp.any(hits, axis=1).astype(bf16).T
    combine = jnp.sum(jnp.where(hits, route_weight[:, :, None], 0.0), axis=1)
    n = EXPERTS * cap
    cuts = 4
    cut = jax.ShapeDtypeStruct((EXPERTS, cuts * cap, width // cuts), bf16)
    hstate, outgoing = call(
        tail_kernel,
        (jax.ShapeDtypeStruct((tok_dev, width), f32), cut),
        (source, parts, residual, norm_gain[None, :], placing),
        smem=1,
        mib=60,
        name="tail",
        scratch_shapes=[pltpu.VMEM((tok_dev, width), f32)],
    )
    rows = call(
        join_kernel,
        jax.ShapeDtypeStruct((n, width), bf16),
        (lax.all_to_all(outgoing, EXP, split_axis=0, concat_axis=0, tiled=True),),
        name="join",
    )

    panels = (gate_weight[0], up_weight[0], down_weight[0], *panels_o)
    near, over = [None] * NZ, [None] * NZ
    near[0], over[0] = rows, other_x(rows)
    done_near, done_over = {}, {}

    def work(*steps):
        blocks = []
        for s in steps:
            if s == 0:
                pieces = [(near[0],), (over[0],)]
            elif s == HALF:
                pieces = [near[s], over[s]]
            else:
                pieces = [(near[s],), (near[NZ - s],), (over[s],), (over[NZ - s],)]
            blocks += [x for piece in pieces for x in piece]
        out = run_experts(jnp.concatenate(blocks, axis=0), panels)
        at = 0
        for s in steps:
            if s in (0, HALF):
                done_near[s], done_over[s] = (out, at), (out, at + n)
                at += 2 * n
            else:
                done_near[s], done_near[NZ - s] = (out, at), (out, at + n)
                done_over[s], done_over[NZ - s] = (out, at + 2 * n), (out, at + 3 * n)
                at += 4 * n
        return out

    na = nb = near[0]
    oa = ob = over[0]
    outs = []

    def ties(place, x, y):
        for where, steps in PLAN:
            if where == place:
                out = work(*steps)
                x, y, _ = lax.optimization_barrier((x, y, out))
        return x, y

    for s in range(1, HALF):
        na, nb = ring_step(*ties(f"n{s}", na, nb))
        oa, ob = ring_step(*ties(f"o{s}", oa, ob))
        near[s], near[NZ - s] = na, nb
        over[s], over[NZ - s] = oa, ob
    near_half, over_half = n // 3, n - n // 3
    na, nb = ties("n4", na, nb)
    near[HALF] = ring_step(na[near_half:], nb[:near_half])
    oa, ob = ties("o4", oa, ob)
    over[HALF] = ring_step(oa[over_half:], ob[:over_half])
    near[HALF] = ties("near", *near[HALF])
    over[HALF] = ties("over", *over[HALF])
    work(*LAST)
    if 0 not in done_near:
        work(0)
    own, at = done_near[0]
    own = own[at : at + 2 * n]
    sums_near = ring_reduce(done_near, n, near_half, *([own] if OWN_LAST else []))
    sums_over = ring_reduce(done_over, n, over_half)
    ready = call(
        close_kernel,
        jax.ShapeDtypeStruct((NX,) + cut.shape, bf16),
        (xl[None], own) + sums_near + sums_over,
        smem=1,
        name="close",
    )
    back = lax.all_to_all(
        ready.reshape((NX * EXPERTS,) + cut.shape[1:]),
        ("xl",) + EXP,
        split_axis=0,
        concat_axis=0,
        tiled=True,
    ).reshape(ready.shape)
    return call(
        mix_kernel,
        jax.ShapeDtypeStruct((tok_dev, width), bf16),
        (hstate, combine, back),
        name="mix",
    )


def solution(mesh):
    fine = Mesh(mesh.devices.reshape(NX, NZ, NC, NH, NY), CTX + EXP)
    placed = (
        P(CTX, EXP),
        P(CTX, EXP),
        P(CTX, EXP),
        P(EXP, CTX),
        P(CTX + EXP, None),
        P(),
        P(EXP, None, CTX),
        P(EXP, None, CTX),
        P(EXP, CTX, None),
        P(CTX + EXP, None),
        P(CTX + EXP, None),
    )
    return jax.shard_map(
        shards, mesh=fine, in_specs=placed, out_specs=P(CTX + EXP, None), check_vma=False
    )
```
